256 devices in a mesh: seq: 16 (over y, x), exp: 16 (over z, core).
Axes of the slice: x: 4, y: 4, z: 8, core: 2. Of those that a mesh axis runs over, the one named last changes fastest.
Arguments:
- queries: bfloat16 [2048, 4096], P('seq', 'exp'), may hold values from -4 to 4
- keyvals: bfloat16 [2048, 2, 512], P('seq'), may hold values from -2.5 to 2.5
- sinks: float32 [64], P('exp'), may hold values from -3 to 3
- out_proj: bfloat16 [4096, 2880], P('exp'), may hold values from -0.75 to 0.75
- residual: bfloat16 [2048, 2880], P('seq', 'exp'), may hold values from -20 to 20
- norm_gain: float32 [2880], P('exp'), may hold values from 0.1 to 1.9
- router_weight: float32 [2880, 32], P('exp'), may hold values from -0.109375 to 0.109375
- route_ids: int32 [2048, 4], P('seq'), may hold values from 0 to 31, all different within a row; in each aligned block of 128 rows (0 to 127, 128 to 255, ...) at most 32 rows name the same one
- expert_in: bfloat16 [256, 2880, 2, 360], P(('seq', 'exp')), may hold values from -0.109375 to 0.109375
- expert_out: bfloat16 [256, 360, 2880], P(('seq', 'exp')), may hold values from -0.109375 to 0.109375
Outputs:
- mixed: bfloat16 [2048, 2880], P('seq', 'exp')
The draws below stay inside these ranges and needn't reach their ends.
Inputs may be any that keep to these rules, and one draw needn't show every extreme that they name: `route_ids`: each row names 4 different experts; within each aligned block of 128 rows no expert is named by more than 32 rows, a bound that some block reaches.
All inputs are finite; a program needn't handle non-finite values.
Results may differ from the reference program's by a relative error of at most 0.015.
Values may be sent and summed in bfloat16 or wider, within the bound.
A program may use at most 128 MiB of HBM per device.

```python
import math
import jax
import jax.numpy as jnp
import numpy as np
from jax import lax

D = 2880
FF = 2880
HEADS = 64
KV_HEADS = 8
HD = 64
WINDOW = 128
TOPK = 4
TOK_SEQ = 128
EXPERTS = 32
SPLIT = 8
UNITS = 360
CAP = 32
TOKENS = 2048
N_SEQ = 16


def draw_residual(key, part):
    key = jax.random.fold_in(key, 7)
    position = jnp.arange(D, dtype=jnp.float32) / D
    column_scale = 0.6 + 1.2 * position
    values_drawn = jnp.clip(jax.random.normal(key, (TOKENS, D), jnp.float32), -4.0, 4.0)
    return (values_drawn * column_scale[None, :]).astype(jnp.bfloat16)


def levels(stream_key, extent, shards, low, largest):
    def one(dim, shards_of):
        heights = jax.random.uniform(jax.random.fold_in(jax.random.fold_in(stream_key, 6), dim), (shards_of,), jnp.float32, low / len(shards), largest / len(shards))
        return jnp.repeat(jnp.exp(heights), extent[dim] // shards_of).reshape((-1,) + (1,) * (len(extent) - dim - 1))

    loudness = one(*shards[0])
    for cut in shards[1:]:
        loudness = loudness * one(*cut)
    return loudness


def routed_block(own_key, own, number, rows, amount, top, bound, skew):
    order = jax.random.permutation(own_key, amount)
    crowded, usual = load_shares(amount, rows * top, bound, skew, True), load_shares(amount, rows * top, bound, skew, False)
    places = jnp.arange(amount)

    def named(lengths, rotation):
        used = int((lengths > 0).sum())
        fixed = max(1, used // 4)
        passed = fixed + (places - fixed + rotation * (used - fixed)) % max(1, amount - fixed)
        return jnp.zeros((amount,), jnp.int32).at[order[jnp.where(places < fixed, places, passed)]].set(jnp.asarray(lengths, jnp.int32))

    lengths = jnp.where(number % 4 == 0, named(crowded, number // 4), named(usual, number - number // 4 - 1))
    mixed = jax.random.permutation(jax.random.fold_in(own, 3), amount)
    source_of, taker = mixed[0:amount // 2 * 2:2], mixed[1:amount // 2 * 2:2]
    slack = jnp.minimum(lengths[source_of] - 1, bound - lengths[taker]) // 2
    slack = jnp.where((source_of == order[0]) | (taker == order[0]) | (lengths[taker] == 0), 0, jnp.maximum(slack, 0))
    passed = jax.random.randint(jax.random.fold_in(own, 4), (amount // 2,), 0, 1 << 20) % (slack + 1)
    lengths = lengths.at[source_of].add(-passed).at[taker].add(passed)
    items = jnp.searchsorted(jnp.cumsum(lengths), jnp.arange(rows * top), side="right").astype(jnp.int32)
    table = items.reshape(top, rows).T
    table = table[jax.random.permutation(jax.random.fold_in(own, 1), rows)]
    rotation = jax.random.randint(jax.random.fold_in(own, 2), (rows, 1), 0, top)
    return jnp.take_along_axis(table, (jnp.arange(top)[None, :] + rotation) % top, axis=1)


def load_shares(amount, total, reach, lean, full):
    loads = [(1 << 20) // math.isqrt(rank ** lean) + 1 for rank in range(1, amount + 1)]
    largest = reach if full else min(reach, max(-(-total // amount), total * loads[0] // sum(loads)))
    least = 1 if total - largest >= amount - 1 else 0
    holding, spare = [largest] + [least] * (amount - 1), total - largest - least * (amount - 1)
    while spare > 0:
        free = [i for i in range(1, amount) if holding[i] < largest] or [i for i in range(1, amount) if holding[i] < reach]
        whole, remaining = sum([loads[i] for i in free]), spare
        for i in free:
            extra = min(reach - holding[i], max(1, remaining * loads[i] // whole), spare)
            holding[i] = holding[i] + extra
            spare = spare - extra
    return np.array(holding)


def gaussian(key, shape, deviation, most, shards=(), kind=jnp.bfloat16):
    factor_of = levels(key, shape, shards, -0.22, 0.18) if shards else 1.0
    values = jax.random.normal(key, shape, jnp.float32) * deviation * factor_of
    return jnp.minimum(jnp.maximum(values, -most), most).astype(kind)


def setup_inputs(seed: int = 0) -> dict:
    seeds = jax.random.split(jax.random.key(seed), 11)
    queries = gaussian(seeds[0], (TOKENS, HEADS * HD), 1.5, 4.0, ((0, 16), (1, 16)))
    keyvals = gaussian(seeds[1], (TOKENS, 2, KV_HEADS * HD), 0.5, 2.5, ((0, 16),))
    sinks = gaussian(seeds[2], (HEADS,), 1.0, 3.0, ((0, 16),), jnp.float32)
    out_proj = gaussian(seeds[3], (HEADS * HD, D), HD ** -0.5, 0.75, ((0, 16),))
    residual = draw_residual(jax.random.fold_in(seeds[10], 71), 0)
    norm_gain = jnp.clip(1.0 + 0.18 * jax.random.normal(seeds[5], (D,), jnp.float32), 0.1, 1.9)
    router_weight = gaussian(seeds[6], (D, EXPERTS), D ** -0.5, 0.109375, ((0, 16),), jnp.float32)
    route_ids_keys = jax.random.split(jax.random.fold_in(seeds[7], 1), TOKENS // TOK_SEQ)
    route_ids_turns = jax.random.permutation(jax.random.fold_in(seeds[7], 3), TOKENS // TOK_SEQ)
    route_ids = jax.vmap(lambda own, number: routed_block(jax.random.fold_in(seeds[7], 2), own, number, TOK_SEQ, EXPERTS, TOPK, CAP, 2))(route_ids_keys, route_ids_turns).reshape((TOKENS, TOPK))
    expert_in = gaussian(seeds[8], (EXPERTS * SPLIT, D, 2, UNITS), D ** -0.5, 0.109375, ((0, 256),))
    expert_out = gaussian(seeds[9], (EXPERTS * SPLIT, UNITS, D), FF ** -0.5, 0.109375, ((0, 256),))
    return {"queries": queries, "keyvals": keyvals, "sinks": sinks, "out_proj": out_proj, "residual": residual, "norm_gain": norm_gain, "router_weight": router_weight, "route_ids": route_ids, "expert_in": expert_in, "expert_out": expert_out}


epsilon = 1e-05

def attend_block(block_index, query_heads, padded_kv, sinks):
    first_row = (block_index * TOK_SEQ).astype(jnp.int32)
    query_block = lax.dynamic_slice_in_dim(query_heads, first_row, TOK_SEQ, 0).astype(jnp.float32)
    key_block = lax.dynamic_slice_in_dim(padded_kv, first_row, TOK_SEQ + WINDOW, 0).astype(jnp.float32)
    scores = jnp.einsum('thd,shd->hts', query_block, key_block[:, 0]) * 0.125
    query_pos = jnp.arange(TOK_SEQ, dtype=jnp.int32)[:, None]
    key_pos = jnp.arange(TOK_SEQ + WINDOW, dtype=jnp.int32)[None, :]
    offset = query_pos - key_pos + WINDOW
    allowed = (offset >= 0) & (offset < WINDOW) & (first_row - WINDOW + key_pos >= 0)
    weights = jnp.where(allowed[None], jnp.exp(scores), jnp.float32(0.0))
    denominator = lax.optimization_barrier(jnp.sum(weights, axis=2)) + jnp.exp(sinks)[:, None]
    probabilities = (weights / denominator[:, :, None]).astype(jnp.bfloat16)
    attended = jnp.einsum('hts,shd->thd', probabilities.astype(jnp.float32), key_block[:, 1])
    return attended.astype(jnp.bfloat16).reshape(TOK_SEQ, HEADS * HD)

def run_expert(operands):
    row_block, weight_in, weight_out = operands
    preact = jnp.einsum('rd,ndgf->rngf', row_block.astype(jnp.float32), weight_in.astype(jnp.float32))
    gate_part = preact[:, :, 0]
    up_part = preact[:, :, 1]
    activated = (gate_part * jax.nn.sigmoid(1.702 * gate_part) * (up_part + 1.0)).astype(jnp.bfloat16)
    pieces = jnp.einsum('rnf,nfd->nrd', activated.astype(jnp.float32), weight_out.astype(jnp.float32))
    rounded = lax.optimization_barrier(pieces.astype(jnp.bfloat16)).astype(jnp.float32)
    return lax.optimization_barrier(jnp.sum(rounded, axis=0))

def reference(queries, keyvals, sinks, out_proj, residual, norm_gain, router_weight, route_ids, expert_in, expert_out):
    group_size = HEADS // KV_HEADS
    blocks = TOKENS // TOK_SEQ
    query_heads = queries.reshape(TOKENS, HEADS, HD)
    expanded = jnp.repeat(keyvals.reshape(TOKENS, 2, KV_HEADS, HD), group_size, axis=2)
    padded_kv = jnp.concatenate([jnp.zeros((WINDOW, 2, HEADS, HD), jnp.bfloat16), expanded], axis=0)
    attended = lax.map(lambda block_index: attend_block(block_index, query_heads, padded_kv, sinks), jnp.arange(blocks, dtype=jnp.int32))
    attended = attended.reshape(TOKENS, HEADS * HD)
    hidden_state = residual.astype(jnp.float32) + jnp.dot(attended, out_proj, preferred_element_type=jnp.float32)
    factor = lax.rsqrt(lax.optimization_barrier(jnp.mean(hidden_state * hidden_state, axis=1)) + epsilon)
    scaled = hidden_state * norm_gain
    normed = (scaled * factor[:, None]).astype(jnp.bfloat16)
    logits = factor[:, None] * jnp.dot(scaled, router_weight, precision=lax.Precision.HIGHEST)
    picked_logits = jnp.take_along_axis(logits, route_ids, axis=1)
    raised = jnp.exp(picked_logits)
    gate_values = raised / lax.optimization_barrier(jnp.sum(raised, axis=1, keepdims=True))
    flat_ids = route_ids.reshape(blocks, TOK_SEQ * TOPK)
    onehot = (flat_ids[:, :, None] == jnp.arange(EXPERTS, dtype=jnp.int32)[None, None, :]).astype(jnp.int32)
    running = jnp.cumsum(onehot, axis=1)
    slot_of = jnp.take_along_axis(running, flat_ids[:, :, None], axis=2)[:, :, 0] - 1
    block_of = jnp.arange(blocks, dtype=jnp.int32)[:, None]
    target = (flat_ids * (N_SEQ * CAP) + block_of * CAP + slot_of).reshape(-1).astype(jnp.int32)
    token_ids = (jnp.arange(TOKENS * TOPK, dtype=jnp.int32) // TOPK).astype(jnp.int32)
    row_table = jnp.full((EXPERTS * N_SEQ * CAP,), TOKENS, jnp.int32).at[target].set(token_ids)
    padded_rows = jnp.concatenate([normed, jnp.zeros((1, D), jnp.bfloat16)], axis=0)
    gathered = padded_rows[row_table].reshape(EXPERTS, N_SEQ * CAP, D)
    panels_in = expert_in.reshape(EXPERTS, SPLIT, D, 2, UNITS)
    panels_out = expert_out.reshape(EXPERTS, SPLIT, UNITS, D)
    outputs = lax.map(run_expert, (gathered, panels_in, panels_out))
    fetched = outputs.reshape(EXPERTS * N_SEQ * CAP, D)[target].reshape(TOKENS, TOPK, D)
    mixture = lax.optimization_barrier(jnp.sum(gate_values[:, :, None] * fetched, axis=1))
    return (hidden_state + mixture).astype(jnp.bfloat16)
```

```python
import jax
import jax.numpy as jnp
from jax import lax
from jax.experimental import pallas as pl
from jax.experimental.pallas import tpu as pltpu
from jax.sharding import PartitionSpec as P

MESH = pl.DeviceIdType.MESH
F32, BF16 = jnp.float32, jnp.bfloat16
D = 2880
UNITS = 360
SHARE = 180
PAD = 192
PAIR = 2 * PAD
HALF = 8 * PAD
TOK = 128
CAP = 32
ROWS = 16 * CAP
EPS = 1e-05
STEPS = (
    (0, 0), (2, 2), (1, 2), (2, 1), (1, 1), (3, 3), (0, 1), (0, 3),
    (2, 3), (3, 2), (0, 2), (2, 0), (1, 3), (3, 1), (1, 0), (3, 0),
)
NT = (((1,), (1,)), ((), ()))


def nt(a, b):
    return lax.dot_general(a, b, NT, preferred_element_type=F32)


def nn(a, b):
    return jnp.dot(a, b, preferred_element_type=F32)


def kernel(
    q_ref, kv_ref, sink_ref, proj_hbm, res_ref, gain_ref, router_ref, route_ref, win_hbm, wout_hbm,
    out_ref,
    proj, stage, kvall, wide, codes, pick, part, sibsend, sibrecv, rsend, rrecv, hid, mine,
    diff, sel, weights, sqsend, sqrecv, lgsend, lgrecv, xg, dsend, x, gates, gthi, gtlo, ghi, glo,
    gacc, uacc, own, csend, crecv, ysend, y, macc, msend, mrecv,
    load_sem, halo_sem, sib_s, sib_r, rs_s, rs_r, sq_s, sq_r, lg_s, lg_r, ag_s, ag_r,
    d_s, d_r, f_s, f_r, c_s, c_r, y_s, y_r, m_s, m_r,
):
    s, e = lax.axis_index("seq"), lax.axis_index("exp")
    z, k = e // 2, lax.rem(e, 2)
    h = e // 8
    other = 1 - k
    sy, sx = s // 4, lax.rem(s, 4)
    ahead = [lax.rem(sy + dy, 4) * 4 + lax.rem(sx + dx, 4) for dy, dx in STEPS]
    behind = [lax.rem(sy + 4 - dy, 4) * 4 + lax.rem(sx + 4 - dx, 4) for dy, dx in STEPS]
    sibling = {"exp": 2 * z + other}
    zup = [lax.rem(z + d, 8) for d in range(8)]
    zdown = [lax.rem(z + 8 - d, 8) for d in range(8)]

    def remote(src, dst, send, recv, device):
        return pltpu.make_async_remote_copy(
            src_ref=src, dst_ref=dst, send_sem=send, recv_sem=recv, device_id=device, device_id_type=MESH
        )

    barrier = pltpu.get_barrier_semaphore()
    for d in range(1, 16):
        pl.semaphore_signal(barrier, inc=1, device_id={"seq": ahead[d]}, device_id_type=MESH)
        pl.semaphore_signal(barrier, inc=1, device_id={"exp": lax.rem(e + d, 16)}, device_id_type=MESH)
    load_proj = pltpu.make_async_copy(proj_hbm, proj, load_sem.at[0])
    load_in = pltpu.make_async_copy(win_hbm, stage.at[pl.ds(0, 2)], load_sem.at[1])
    load_out = pltpu.make_async_copy(wout_hbm, stage.at[2], load_sem.at[2])
    load_proj.start()
    load_in.start()
    load_out.start()
    kvall[TOK:, :] = kv_ref[...]
    pl.semaphore_wait(barrier, 30)

    halo = remote(kv_ref, kvall.at[pl.ds(0, TOK)], halo_sem.at[0], halo_sem.at[1], {"seq": lax.rem(s + 1, 16)})
    halo.start()

    expert = lax.broadcasted_iota(jnp.int32, (32, TOK), 0)
    named = route_ref[0:1, :] == expert
    for j in range(1, 4):
        named = named | (route_ref[j : j + 1, :] == expert)
    named = jnp.where(named, jnp.float32(1.0), jnp.float32(0.0))
    before = jnp.where(
        lax.broadcasted_iota(jnp.int32, (TOK, TOK), 0) < lax.broadcasted_iota(jnp.int32, (TOK, TOK), 1),
        jnp.float32(1.0), jnp.float32(0.0),
    ).astype(BF16)
    rank = nn(named.astype(BF16), before)
    codes[...] = jnp.where(named > 0.0, rank, jnp.float32(-1.0))
    row = lax.broadcasted_iota(jnp.int32, (CAP, TOK), 0).astype(F32)
    for d in range(16):
        code = codes[pl.ds(2 * ahead[d] + h, 1), :]
        pick[CAP * d : CAP * (d + 1), :] = jnp.where(code == row, jnp.float32(1.0), jnp.float32(0.0)).astype(BF16)
    weights[...] = jnp.zeros_like(weights)

    halo.wait_recv()
    kvf = kvall[...].astype(F32)
    turned = pltpu.roll(kvf, 64, 1)
    low = lax.broadcasted_iota(jnp.int32, (2 * TOK, TOK), 1) < 64
    zero = jnp.zeros_like(kvf)
    keys = [jnp.where(low, kvf, zero).astype(BF16), jnp.where(low, zero, turned).astype(BF16)]
    values = [jnp.where(low, turned, zero).astype(BF16), jnp.where(low, zero, kvf).astype(BF16)]
    qpos = lax.broadcasted_iota(jnp.int32, (TOK, 2 * TOK), 0)
    kpos = lax.broadcasted_iota(jnp.int32, (TOK, 2 * TOK), 1)
    offset = qpos - kpos + TOK
    allowed = (offset >= 0) & (offset < TOK) & (kpos >= jnp.where(s > 0, 0, TOK))
    for pair in range(2):
        query = q_ref[:, 128 * pair : 128 * (pair + 1)]
        total = None
        for side in range(2):
            head = 2 * pair + side
            score = nt(query, keys[side]) * 0.125
            weight = jnp.where(allowed, jnp.exp(score), jnp.float32(0.0))
            denominator = jnp.sum(weight, axis=1, keepdims=True) + jnp.exp(sink_ref[0:1, head : head + 1])
            term = nn((weight / denominator).astype(BF16), values[side])
            total = term if total is None else total + term
        wide[:, 128 * pair : 128 * (pair + 1)] = total.astype(BF16)

    load_proj.wait()
    attended = wide[...]

    def project(i, carry):
        r = pl.multiple_of(i * 576, 576)
        part[pl.ds(r, 576), :] = nt(proj[pl.ds(r, 576), :], attended)
        return carry

    lax.fori_loop(0, 5, project, 0)
    part[D : D + 16, :] = jnp.zeros((16, TOK), F32)
    order = (1, 2, 3, 4, 5, 6, 7, 0)
    first, second = [None] * 8, [None] * 8
    for d in order:
        sibsend[d] = part[pl.ds(SHARE * (2 * zup[d] + other), PAD), :].astype(BF16)
        first[d] = remote(sibsend.at[d], sibrecv.at[d], sib_s.at[d], sib_r.at[d], sibling)
        first[d].start()
    for d in order:
        first[d].wait_recv()
        pair_sum = part[pl.ds(SHARE * (2 * zup[d] + k), PAD), :] + sibrecv[d].astype(F32)
        if d == 0:
            mine[...] = pair_sum
        else:
            rsend[d] = pair_sum.astype(BF16)
            second[d] = remote(rsend.at[d], rrecv.at[d], rs_s.at[d], rs_r.at[d], {"exp": 2 * zup[d] + k})
            second[d].start()

    load_in.wait()
    load_out.wait()
    ji = lax.broadcasted_iota(jnp.int32, (2 * PAIR, PAIR), 1)
    di = lax.broadcasted_iota(jnp.int32, (2 * PAIR, PAIR), 0) - ji
    di = jnp.where(ji < SHARE, di, -9999)
    ji2 = (ji >= PAD) & (ji < PAD + SHARE)
    di2 = lax.broadcasted_iota(jnp.int32, (2 * PAIR, PAIR), 0) - ji - (2 * SHARE - PAD)
    diff[...] = jnp.where(ji2, di2, di)

    def spread(t, carry):
        q, p = t // 2, lax.rem(t, 2)
        start = 4 * SHARE * q + SHARE * p
        w0 = (start // 128) * 128
        sel[...] = jnp.where(diff[...] == start - w0, jnp.float32(1.0), jnp.float32(0.0)).astype(BF16)

        def matrix(m, c):
            block = stage[m, :, pl.ds(pl.multiple_of(w0, 128), 2 * PAIR)]
            weights[m, p, 0:UNITS, pl.ds(pl.multiple_of(q * PAIR, 128), PAIR)] = nn(block, sel[...]).astype(BF16)
            return c

        return lax.fori_loop(0, 3, matrix, carry)

    lax.fori_loop(0, 7, spread, 0)
    sel[...] = jnp.where(diff[...] == 36, jnp.float32(1.0), jnp.float32(0.0)).astype(BF16)

    def last(m, c):
        block = stage[m, :, 2304:D]
        weights[m, 1, 0:UNITS, 3 * PAIR : 4 * PAIR] = nn(block, sel[0:576, :]).astype(BF16)
        return c

    lax.fori_loop(0, 3, last, 0)

    total = mine[...]
    for d in range(1, 8):
        second[d].wait_recv()
        total = total + rrecv[d].astype(F32)
    hid[SHARE - 4 :, :] = jnp.zeros((PAD - SHARE + 4, TOK), F32)
    hid[0:SHARE, :] = res_ref[...].astype(F32) + total[0:SHARE, :]
    state = hid[...]
    sqsend[...] = jnp.broadcast_to(jnp.sum(state * state, axis=0, keepdims=True), (8, TOK))
    squares = [None] * 16
    for d in range(1, 16):
        device = {"exp": lax.rem(e + d, 16)}
        squares[d] = remote(sqsend, sqrecv.at[d], sq_s.at[d], sq_r.at[d], device)
        squares[d].start()
    diagonal = lax.broadcasted_iota(jnp.int32, (PAD, SHARE), 0) == lax.broadcasted_iota(jnp.int32, (PAD, SHARE), 1)
    gain = jnp.sum(jnp.where(diagonal, gain_ref[...], jnp.float32(0.0)), axis=1, keepdims=True)
    scaled = state * gain
    xg[z] = scaled.astype(BF16)
    gather = [None] * 8
    for d in range(1, 8):
        gather[d] = remote(xg.at[z], xg.at[z], ag_s.at[d], ag_r.at[d], {"exp": 2 * zup[d] + k})
        gather[d].start()
    lgsend[...] = jnp.dot(
        router_ref[...], scaled[0:SHARE, :], precision=lax.Precision.HIGHEST, preferred_element_type=F32
    )
    logit_copies = [None] * 16
    for d in range(1, 16):
        device = {"exp": lax.rem(e + d, 16)}
        logit_copies[d] = remote(lgsend, lgrecv.at[d], lg_s.at[d], lg_r.at[d], device)
        logit_copies[d].start()
    square = sqsend[0:1, :]
    for d in range(1, 16):
        squares[d].wait_recv()
        square = square + sqrecv[d, 0:1, :]
    factor = lax.rsqrt(square / D + EPS)

    for d in range(1, 8):
        slot = zdown[d]
        remote(xg.at[slot], xg.at[slot], ag_s.at[d], ag_r.at[d], {"exp": 2 * zup[d] + k}).wait_recv()
    sends = [None] * 16
    for g in range(4):
        r = slice(TOK * g, TOK * (g + 1))
        chosen = pick[r, :]
        scale = jnp.sum(chosen.astype(F32) * factor, axis=1, keepdims=True)
        for q in range(4):
            features = xg[2 * q : 2 * q + 2].reshape(PAIR, TOK)
            dsend[r, PAIR * q : PAIR * (q + 1)] = (nt(chosen, features) * scale).astype(BF16)
        for d in range(4 * g, 4 * g + 4):
            if d == 0:
                x[k, 0:CAP, :] = dsend[0:CAP, :]
            else:
                sends[d] = remote(
                    dsend.at[pl.ds(CAP * d, CAP)], x.at[k, pl.ds(CAP * d, CAP)], d_s.at[d], d_r.at[d], {"seq": ahead[d]}
                )
                sends[d].start()

    logits = lgsend[...]
    for d in range(1, 16):
        logit_copies[d].wait_recv()
        logits = logits + lgrecv[d]
    raised = jnp.where(named > 0.0, jnp.exp(logits * factor), jnp.float32(0.0))
    gates[...] = raised / jnp.sum(raised, axis=0, keepdims=True)
    for d in range(16):
        r = slice(CAP * d, CAP * (d + 1))
        gate = gates[pl.ds(2 * ahead[d] + h, 1), :] * pick[r, :].astype(F32)
        gthi[r, :] = gate.astype(BF16)
        gtlo[r, :] = (gate - gate.astype(BF16).astype(F32)).astype(BF16)
    unit = jnp.where(
        lax.broadcasted_iota(jnp.int32, (TOK, TOK), 0) == lax.broadcasted_iota(jnp.int32, (TOK, TOK), 1),
        jnp.float32(1.0), jnp.float32(0.0),
    ).astype(BF16)
    ghi[...] = nt(unit, gthi[...]).astype(BF16)
    glo[...] = nt(unit, gtlo[...]).astype(BF16)

    backs = [None] * 16
    forwards = [None] * 16
    pairs = [None] * 2
    for g in range(2):
        base = 256 * g
        r = slice(base, base + 256)
        for d in range(8 * g, 8 * g + 8):
            piece = pl.ds(CAP * d, CAP)
            if d > 0:
                sends[d].wait_recv()
            forwards[d] = remote(x.at[k, piece], x.at[k, piece], f_s.at[d], f_r.at[d], sibling)
            forwards[d].start()
        gacc[...] = nt(x[k, r, :], weights[0, k])
        uacc[...] = nt(x[k, r, :], weights[1, k])
        for d in range(8 * g, 8 * g + 8):
            piece = pl.ds(CAP * d, CAP)
            remote(x.at[other, piece], x.at[other, piece], f_s.at[d], f_r.at[d], sibling).wait_recv()
        gate = gacc[...] + nt(x[other, r, :], weights[0, other])
        up = uacc[...] + nt(x[other, r, :], weights[1, other])
        activated = (gate * jax.nn.sigmoid(1.702 * gate) * (up + 1.0)).astype(BF16)
        csend[r, :] = nn(activated, weights[2, other]).astype(BF16)
        pairs[g] = remote(csend.at[pl.ds(base, 256)], crecv.at[pl.ds(base, 256)], c_s.at[g], c_r.at[g], sibling)
        pairs[g].start()
        own[...] = nn(activated, weights[2, k])
        pairs[g].wait_recv()
        for d in range(8 * g, 8 * g + 8):
            b = slice(CAP * d, CAP * (d + 1))
            block = (own[CAP * d - base : CAP * (d + 1) - base, :] + crecv[b, :].astype(F32)).astype(BF16)
            if d == 0:
                y[b, :] = block
            else:
                ysend[b, :] = block
                piece = pl.ds(CAP * d, CAP)
                backs[d] = remote(ysend.at[piece], y.at[piece], y_s.at[d], y_r.at[d], {"seq": behind[d]})
                backs[d].start()

    for g in range(2):
        r = slice(256 * g, 256 * (g + 1))
        for d in range(8 * g, 8 * g + 8):
            if d > 0:
                backs[d].wait_recv()
        term = nn(ghi[:, r], y[r, :]) + nn(glo[:, r], y[r, :])
        if g == 0:
            macc[...] = term
        else:
            macc[...] = macc[...] + term
    unit = jnp.where(
        lax.broadcasted_iota(jnp.int32, (PAIR, PAIR), 0) == lax.broadcasted_iota(jnp.int32, (PAIR, PAIR), 1),
        jnp.float32(1.0), jnp.float32(0.0),
    ).astype(BF16)
    for q in range(4):
        turned = nt(unit, macc[:, PAIR * q : PAIR * (q + 1)].astype(BF16))
        msend[2 * q : 2 * q + 2] = turned.astype(BF16).reshape(2, PAD, TOK)
    finals = [None] * 8
    for d in range(1, 8):
        finals[d] = remote(msend.at[zup[d]], mrecv.at[d], m_s.at[d], m_r.at[d], {"exp": 2 * zup[d] + k})
        finals[d].start()
    total = hid[...] + msend[z].astype(F32)
    for d in range(1, 8):
        finals[d].wait_recv()
        total = total + mrecv[d].astype(F32)
    out_ref[...] = total[0:SHARE, :].astype(BF16)

    halo.wait_send()
    for d in range(8):
        first[d].wait_send()
    for d in range(1, 8):
        second[d].wait_send()
        gather[d].wait_send()
        finals[d].wait_send()
    for d in range(1, 16):
        squares[d].wait_send()
        logit_copies[d].wait_send()
        sends[d].wait_send()
        backs[d].wait_send()
    for d in range(16):
        forwards[d].wait_send()
    for g in range(2):
        pairs[g].wait_send()


def vmem(*shape, dtype=BF16):
    return pltpu.VMEM(shape, dtype)


def body(
    queries, keyvals, sinks, out_proj, residual, norm_gain, router_weight, route_ids, expert_in, expert_out
):
    z = lax.axis_index("exp") // 2
    kv = lax.dynamic_slice(keyvals, (0, 0, 64 * z), (TOK, 2, 64)).reshape(TOK, TOK)
    local = pl.BlockSpec(memory_space=pltpu.VMEM)
    far = pl.BlockSpec(memory_space=pltpu.HBM)
    sems = lambda n: pltpu.SemaphoreType.DMA((n,))
    mixed = pl.pallas_call(
        kernel,
        out_shape=jax.ShapeDtypeStruct((SHARE, TOK), BF16),
        in_specs=[local, local, local, far, local, local, local, local, far, far],
        out_specs=local,
        scratch_shapes=[
            vmem(D, 256),
            vmem(3, UNITS, D),
            vmem(2 * TOK, TOK),
            vmem(TOK, 256),
            vmem(32, TOK, dtype=F32),
            vmem(ROWS, TOK),
            vmem(D + 16, TOK, dtype=F32),
            vmem(8, PAD, TOK),
            vmem(8, PAD, TOK),
            vmem(8, PAD, TOK),
            vmem(8, PAD, TOK),
            vmem(PAD, TOK, dtype=F32),
            vmem(PAD, TOK, dtype=F32),
            vmem(2 * PAIR, PAIR, dtype=jnp.int32),
            vmem(2 * PAIR, PAIR),
            vmem(3, 2, PAIR, HALF),
            vmem(8, TOK, dtype=F32),
            vmem(16, 8, TOK, dtype=F32),
            vmem(32, TOK, dtype=F32),
            vmem(16, 32, TOK, dtype=F32),
            vmem(8, PAD, TOK),
            vmem(ROWS, HALF),
            vmem(2, ROWS, HALF),
            vmem(32, TOK, dtype=F32),
            vmem(ROWS, TOK),
            vmem(ROWS, TOK),
            vmem(TOK, ROWS),
            vmem(TOK, ROWS),
            vmem(256, PAIR, dtype=F32),
            vmem(256, PAIR, dtype=F32),
            vmem(256, HALF, dtype=F32),
            vmem(ROWS, HALF),
            vmem(ROWS, HALF),
            vmem(ROWS, HALF),
            vmem(ROWS, HALF),
            vmem(TOK, HALF, dtype=F32),
            vmem(8, PAD, TOK),
            vmem(8, PAD, TOK),
            sems(3), sems(2), sems(8), sems(8), sems(8), sems(8), sems(16), sems(16), sems(16), sems(16),
            sems(8), sems(8), sems(16), sems(16), sems(16), sems(16), sems(2), sems(2), sems(16), sems(16),
            sems(8), sems(8),
        ],
        compiler_params=pltpu.CompilerParams(
            collective_id=0, has_side_effects=True, vmem_limit_bytes=56 * 2**20
        ),
        name="layer",
    )(
        queries,
        kv,
        sinks.reshape(1, 4),
        out_proj.T,
        residual.T,
        norm_gain.reshape(1, SHARE),
        router_weight.T,
        route_ids.T,
        jnp.transpose(expert_in[0], (1, 2, 0)),
        expert_out[0],
    )
    return mixed.T


def solution(mesh):
    return jax.shard_map(
        body,
        mesh=mesh,
        in_specs=(
            P("seq", "exp"),
            P("seq", None, None),
            P("exp"),
            P("exp", None),
            P("seq", "exp"),
            P("exp"),
            P("exp", None),
            P("seq", None),
            P(("seq", "exp"), None, None, None),
            P(("seq", "exp"), None, None),
        ),
        out_specs=P("seq", "exp"),
        check_vma=False,
    )
```

```python
import jax
import jax.numpy as jnp
from jax import lax
from jax.experimental import pallas as pl
from jax.experimental.pallas import tpu as pltpu
from jax.sharding import PartitionSpec as P

MESH = pl.DeviceIdType.MESH
F32, BF16 = jnp.float32, jnp.bfloat16
D = 2880
UNITS = 360
SHARE = 180
PAD = 192
PAIR = 2 * PAD
HALF = 8 * PAD
TOK = 128
CAP = 32
ROWS = 16 * CAP
EPS = 1e-05
STEPS = (
    (0, 0), (2, 2), (1, 2), (3, 2), (2, 1), (2, 3), (1, 1), (3, 3),
    (1, 3), (3, 1), (0, 2), (2, 0), (0, 1), (1, 0), (0, 3), (3, 0),
)
NT = (((1,), (1,)), ((), ()))


def nt(a, b):
    return lax.dot_general(a, b, NT, preferred_element_type=F32)


def nn(a, b):
    return jnp.dot(a, b, preferred_element_type=F32)


def kernel(
    q_ref, kv_ref, sink_ref, proj_hbm, res_ref, gain_ref, router_ref, route_ref, win_hbm, wout_hbm,
    out_ref,
    proj, stage, kvall, wide, codes, pick, part, sibsend, sibrecv, rsend, rrecv, hid, mine,
    diff, sel, weights, sqsend, sqrecv, lgsend, lgsib, lgsum, lgrecv, xg, esend, ssend, x, gates, gthi, gtlo, ghi, glo,
    gacc, uacc, owns, owne, csend, crecv, psend, precv, yssend, yesend, ys, ye, maccs, macce, msends, msende, mrecv,
    load_sem, halo_sem, sib_s, sib_r, rs_s, rs_r, sq_s, sq_r, lg_s, lg_r, ag_s, ag_r,
    de_s, de_r, ds_s, ds_r, pf_s, pf_r, f_s, f_r, c_s, c_r, p_s, p_r, ys_s, ys_r, ye_s, ye_r, m_s, m_r,
):
    s, e = lax.axis_index("seq"), lax.axis_index("exp")
    z, k = e // 2, lax.rem(e, 2)
    h, b, mid = e // 8, lax.rem(z, 2), lax.rem(z // 2, 2)
    other = 1 - k
    sy, sx = s // 4, lax.rem(s, 4)
    ahead = [lax.rem(sy + dy, 4) * 4 + lax.rem(sx + dx, 4) for dy, dx in STEPS]
    behind = [lax.rem(sy + 4 - dy, 4) * 4 + lax.rem(sx + 4 - dx, 4) for dy, dx in STEPS]
    sibling = {"exp": 2 * z + other}
    zup = [lax.rem(z + d, 8) for d in range(8)]
    mate = z + 1 - 2 * b
    partner = {"exp": 2 * mate + k}
    far_half = 4 * (1 - h)
    group = 2 * h + b
    lane_e = pl.multiple_of(PAIR * group, 128)
    lane_p = pl.multiple_of(PAIR * (2 * h + 1 - b), 128)
    lane_s = pl.multiple_of(2 * PAIR * (1 - h), 128)
    lane_o = pl.multiple_of(2 * PAIR * h, 128)

    def remote(src, dst, send, recv, device):
        return pltpu.make_async_remote_copy(
            src_ref=src, dst_ref=dst, send_sem=send, recv_sem=recv, device_id=device, device_id_type=MESH
        )

    barrier = pltpu.get_barrier_semaphore()
    for d in range(1, 16):
        pl.semaphore_signal(barrier, inc=1, device_id={"seq": ahead[d]}, device_id_type=MESH)
        pl.semaphore_signal(barrier, inc=1, device_id={"exp": lax.rem(e + d, 16)}, device_id_type=MESH)
    load_proj = pltpu.make_async_copy(proj_hbm, proj, load_sem.at[0])
    load_in = pltpu.make_async_copy(win_hbm, stage.at[pl.ds(0, 2)], load_sem.at[1])
    load_out = pltpu.make_async_copy(wout_hbm, stage.at[2], load_sem.at[2])
    load_proj.start()
    load_in.start()
    load_out.start()
    kvall[TOK:, :] = kv_ref[...]

    expert = lax.broadcasted_iota(jnp.int32, (32, TOK), 0)
    named = route_ref[0:1, :] == expert
    for j in range(1, 4):
        named = named | (route_ref[j : j + 1, :] == expert)
    named = jnp.where(named, jnp.float32(1.0), jnp.float32(0.0))
    before = jnp.where(
        lax.broadcasted_iota(jnp.int32, (TOK, TOK), 0) < lax.broadcasted_iota(jnp.int32, (TOK, TOK), 1),
        jnp.float32(1.0), jnp.float32(0.0),
    ).astype(BF16)
    rank = nn(named.astype(BF16), before)
    codes[...] = jnp.where(named > 0.0, rank, jnp.float32(-1.0))
    row = lax.broadcasted_iota(jnp.int32, (CAP, TOK), 0).astype(F32)
    for d in range(16):
        code = codes[pl.ds(2 * ahead[d] + h, 1), :]
        pick[CAP * d : CAP * (d + 1), :] = jnp.where(code == row, jnp.float32(1.0), jnp.float32(0.0)).astype(BF16)

    pl.semaphore_wait(barrier, 30)
    halo = remote(kv_ref, kvall.at[pl.ds(0, TOK)], halo_sem.at[0], halo_sem.at[1], {"seq": lax.rem(s + 1, 16)})
    halo.start()
    weights[...] = jnp.zeros_like(weights)

    low = lax.broadcasted_iota(jnp.int32, (TOK, TOK), 1) < 64

    def sides(ref_part):
        kvf = ref_part.astype(F32)
        turned = pltpu.roll(kvf, 64, 1)
        zero = jnp.zeros_like(kvf)
        keys = [jnp.where(low, kvf, zero).astype(BF16), jnp.where(low, zero, turned).astype(BF16)]
        values = [jnp.where(low, turned, zero).astype(BF16), jnp.where(low, zero, kvf).astype(BF16)]
        return keys, values

    qpos = lax.broadcasted_iota(jnp.int32, (TOK, TOK), 0)
    kpos = lax.broadcasted_iota(jnp.int32, (TOK, TOK), 1)
    keys, values = sides(kvall[TOK:, :])
    new = []
    for head in range(4):
        query = q_ref[:, 128 * (head // 2) : 128 * (head // 2 + 1)]
        score = nt(query, keys[head % 2]) * 0.125
        new.append(jnp.where(kpos <= qpos, jnp.exp(score), jnp.float32(0.0)))
    new_values = values
    halo.wait_recv()
    keys, values = sides(kvall[0:TOK, :])
    allowed = kpos > qpos + jnp.where(s > 0, 0, TOK)
    for pair in range(2):
        query = q_ref[:, 128 * pair : 128 * (pair + 1)]
        total = None
        for side in range(2):
            head = 2 * pair + side
            score = nt(query, keys[side]) * 0.125
            weight = jnp.where(allowed, jnp.exp(score), jnp.float32(0.0))
            denominator = jnp.sum(weight + new[head], axis=1, keepdims=True) + jnp.exp(
                sink_ref[0:1, head : head + 1]
            )
            scale = 1.0 / denominator
            term = nn((weight * scale).astype(BF16), values[side])
            term = term + nn((new[head] * scale).astype(BF16), new_values[side])
            total = term if total is None else total + term
        wide[:, 128 * pair : 128 * (pair + 1)] = total.astype(BF16)

    load_proj.wait()
    attended = wide[...]

    def project(i, carry):
        r = pl.multiple_of(i * 576, 576)
        part[pl.ds(r, 576), :] = nt(proj[pl.ds(r, 576), :], attended)
        return carry

    lax.fori_loop(0, 5, project, 0)
    part[D : D + 16, :] = jnp.zeros((16, TOK), F32)
    order = (4, 3, 5, 2, 6, 1, 7, 0)
    first, second = [None] * 8, [None] * 8
    for d in order:
        sibsend[d] = part[pl.ds(SHARE * (2 * zup[d] + other), PAD), :].astype(BF16)
        first[d] = remote(sibsend.at[d], sibrecv.at[d], sib_s.at[d], sib_r.at[d], sibling)
        first[d].start()
    for d in order:
        first[d].wait_recv()
        pair_sum = part[pl.ds(SHARE * (2 * zup[d] + k), PAD), :] + sibrecv[d].astype(F32)
        if d == 0:
            mine[...] = pair_sum
        else:
            rsend[d] = pair_sum.astype(BF16)
            second[d] = remote(rsend.at[d], rrecv.at[d], rs_s.at[d], rs_r.at[d], {"exp": 2 * zup[d] + k})
            second[d].start()

    load_in.wait()
    ji = lax.broadcasted_iota(jnp.int32, (2 * PAIR, PAIR), 1)
    di = lax.broadcasted_iota(jnp.int32, (2 * PAIR, PAIR), 0) - ji
    di = jnp.where(ji < SHARE, di, -9999)
    ji2 = (ji >= PAD) & (ji < PAD + SHARE)
    di2 = lax.broadcasted_iota(jnp.int32, (2 * PAIR, PAIR), 0) - ji - (2 * SHARE - PAD)
    diff[...] = jnp.where(ji2, di2, di)

    def spread(first_matrix, count):
        def block(t, carry):
            q, p = t // 2, lax.rem(t, 2)
            start = 4 * SHARE * q + SHARE * p
            w0 = (start // 128) * 128
            sel[...] = jnp.where(diff[...] == start - w0, jnp.float32(1.0), jnp.float32(0.0)).astype(BF16)

            def matrix(m, c):
                window = stage[m, :, pl.ds(pl.multiple_of(w0, 128), 2 * PAIR)]
                lanes = pl.ds(pl.multiple_of(q * PAIR, 128), PAIR)
                weights[m, p, 0:UNITS, lanes] = nn(window, sel[...]).astype(BF16)
                return c

            return lax.fori_loop(first_matrix, first_matrix + count, matrix, carry)

        def last(m, c):
            window = stage[m, :, 2304:D]
            weights[m, 1, 0:UNITS, 3 * PAIR : 4 * PAIR] = nn(window, sel[0:576, :]).astype(BF16)
            return c

        lax.fori_loop(0, 7, block, 0)
        sel[...] = jnp.where(diff[...] == 36, jnp.float32(1.0), jnp.float32(0.0)).astype(BF16)
        lax.fori_loop(first_matrix, first_matrix + count, last, 0)

    spread(0, 2)

    total = mine[...]
    for d in (1, 7, 2, 6, 3, 5, 4):
        second[d].wait_recv()
        total = total + rrecv[d].astype(F32)
    hid[SHARE - 4 :, :] = jnp.zeros((PAD - SHARE + 4, TOK), F32)
    hid[0:SHARE, :] = res_ref[...].astype(F32) + total[0:SHARE, :]
    state = hid[...]
    diagonal = lax.broadcasted_iota(jnp.int32, (PAD, SHARE), 0) == lax.broadcasted_iota(jnp.int32, (PAD, SHARE), 1)
    gain = jnp.sum(jnp.where(diagonal, gain_ref[...], jnp.float32(0.0)), axis=1, keepdims=True)
    scaled = state * gain
    xg[z] = scaled.astype(BF16)
    sqsend[...] = jnp.sum(state * state, axis=0, keepdims=True)
    gather = [
        remote(xg.at[z], xg.at[z], ag_s.at[0], ag_r.at[0], partner),
        remote(xg.at[z], xg.at[z], ag_s.at[1], ag_r.at[1 + b], {"exp": 2 * (4 * h + 2 - mid) + k}),
    ]
    for j in range(4):
        device = {"exp": 2 * (far_half + j) + k}
        gather.append(remote(xg.at[z], xg.at[z], ag_s.at[2 + j], ag_r.at[3 + lax.rem(z, 4)], device))
    gather[0].start()
    gather[1].start()
    squares = [None] * 16
    for d in range(1, 16):
        device = {"exp": lax.rem(e + d, 16)}
        squares[d] = remote(sqsend, sqrecv.at[d], sq_s.at[d], sq_r.at[d], device)
        squares[d].start()
    for j in range(4):
        gather[2 + j].start()
    lgsend[...] = jnp.dot(
        router_ref[...], scaled[0:SHARE, :], precision=lax.Precision.HIGHEST, preferred_element_type=F32
    )
    logit_copies = [remote(lgsend, lgsib, lg_s.at[0], lg_r.at[0], sibling)]
    logit_copies[0].start()
    def arrived(slot, sem):
        remote(xg.at[slot], xg.at[slot], ag_s.at[0], ag_r.at[sem], partner).wait_recv()

    arrived(mate, 0)

    @pl.when(b != mid)
    def _():
        arrived(4 * h + 2 * (1 - mid), 1)
        arrived(4 * h + 2 * (1 - mid) + 1, 2)

    to_e, to_s = [None] * 16, [None] * 16
    features = xg[pl.ds(2 * group, 2)].reshape(PAIR, TOK)
    for g in range(4):
        r = slice(TOK * g, TOK * (g + 1))
        chosen = pick[r, :]
        esend[r, :] = nt(chosen, features).astype(BF16)
        for d in range(4 * g, 4 * g + 4):
            if d == 0:
                x[k, 0:CAP, pl.ds(lane_e, PAIR)] = esend[0:CAP, :]
            else:
                piece = pl.ds(CAP * d, CAP)
                target = x.at[k, piece, pl.ds(lane_e, PAIR)]
                to_e[d] = remote(esend.at[piece], target, de_s.at[d], de_r.at[d], {"seq": ahead[d]})
                to_e[d].start()

    passed, forwards = [None] * 4, [None] * 12

    def pass_on(g):
        for d in range(4 * g, 4 * g + 4):
            if d > 0:
                to_e[d].wait_recv()
        block = x.at[k, pl.ds(TOK * g, TOK), pl.ds(lane_e, PAIR)]
        passed[g] = remote(block, block, pf_s.at[g], pf_r.at[g], partner)
        passed[g].start()
        forwards[g] = remote(block, block, f_s.at[g], f_r.at[g], sibling)
        forwards[g].start()

    pass_on(0)
    pass_on(1)
    for j in range(4):
        arrived(far_half + j, 3 + j)
    square = sqsend[...]
    for d in range(1, 16):
        squares[d].wait_recv()
        square = square + sqrecv[d]
    factor = lax.rsqrt(square / D + EPS)
    high = factor.astype(BF16).astype(F32)
    ti = lax.broadcasted_iota(jnp.int32, (16, TOK), 0)
    tail = xg[far_half, PAD - 16 :, :].astype(F32)
    tail = jnp.where(ti == 4, high, jnp.where(ti == 5, factor - high, tail))
    xg[far_half, PAD - 16 :, :] = tail.astype(BF16)
    for g in range(4):
        r = slice(TOK * g, TOK * (g + 1))
        for q in range(2):
            features = xg[pl.ds(far_half + 2 * q, 2)].reshape(PAIR, TOK)
            ssend[r, PAIR * q : PAIR * (q + 1)] = nt(pick[r, :], features).astype(BF16)
        for d in range(4 * g, 4 * g + 4):
            if d == 0:
                x[k, 0:CAP, pl.ds(lane_s, 2 * PAIR)] = ssend[0:CAP, :]
            else:
                piece = pl.ds(CAP * d, CAP)
                target = x.at[k, piece, pl.ds(lane_s, 2 * PAIR)]
                to_s[d] = remote(ssend.at[piece], target, ds_s.at[d], ds_r.at[d], {"seq": ahead[d]})
                to_s[d].start()
    pass_on(2)
    pass_on(3)

    logit_copies[0].wait_recv()
    lgsum[...] = lgsend[...] + lgsib[...]
    for d in range(1, 8):
        device = {"exp": 2 * zup[d] + k}
        logit_copies.append(remote(lgsum, lgrecv.at[d], lg_s.at[d], lg_r.at[d], device))
        logit_copies[d].start()
    unit = jnp.where(
        lax.broadcasted_iota(jnp.int32, (TOK, TOK), 0) == lax.broadcasted_iota(jnp.int32, (TOK, TOK), 1),
        jnp.float32(1.0), jnp.float32(0.0),
    ).astype(BF16)

    load_out.wait()
    spread(2, 1)

    def make_gates():
        logits = lgsum[...]
        for d in range(1, 8):
            logit_copies[d].wait_recv()
            logits = logits + lgrecv[d]
        raised = jnp.where(named > 0.0, jnp.exp(logits * factor), jnp.float32(0.0))
        gates[...] = raised / jnp.sum(raised, axis=0, keepdims=True)
        for d in range(16):
            r = slice(CAP * d, CAP * (d + 1))
            gate = gates[pl.ds(2 * ahead[d] + h, 1), :] * pick[r, :].astype(F32)
            gthi[r, :] = gate.astype(BF16)
            gtlo[r, :] = (gate - gate.astype(BF16).astype(F32)).astype(BF16)
        ghi[...] = nt(unit, gthi[...]).astype(BF16)
        glo[...] = nt(unit, gtlo[...]).astype(BF16)

    back_s, back_e, pairs, swaps = [None] * 16, [None] * 16, [None] * 4, [None] * 4

    def finish_group(g):
        for d in range(8 * g, 8 * g + 8):
            if d % 4 == 0:
                swaps[d // 4].wait_recv()
            blk = slice(CAP * d, CAP * (d + 1))
            block = owne[blk, pl.ds(pl.multiple_of(PAIR * b, 128), PAIR)] + precv[blk, :].astype(F32)
            if d == 0:
                ye[blk, :] = block.astype(BF16)
            else:
                yesend[blk, :] = block.astype(BF16)
                piece = pl.ds(CAP * d, CAP)
                back_e[d] = remote(yesend.at[piece], ye.at[piece], ye_s.at[d], ye_r.at[d], {"seq": behind[d]})
                back_e[d].start()

    def sum_shared(g):
        r = slice(256 * g, 256 * (g + 1))
        for d in range(8 * g, 8 * g + 8):
            if d > 0:
                back_s[d].wait_recv()
        return nn(ghi[:, r], ys[r, :]) + nn(glo[:, r], ys[r, :])

    for g in range(2):
        base = 256 * g
        r = slice(base, base + 256)
        for m in (2 * g, 2 * g + 1):
            for d in range(4 * m, 4 * m + 4):
                if d > 0:
                    to_s[d].wait_recv()
            block = x.at[k, pl.ds(TOK * m, TOK), pl.ds(lane_s, 2 * PAIR)]
            forwards[4 + m] = remote(block, block, f_s.at[4 + m], f_r.at[4 + m], sibling)
            forwards[4 + m].start()
        for m in (2 * g, 2 * g + 1):
            block = x.at[k, pl.ds(TOK * m, TOK), pl.ds(lane_p, PAIR)]
            remote(block, block, pf_s.at[m], pf_r.at[m], partner).wait_recv()
            forwards[8 + m] = remote(block, block, f_s.at[8 + m], f_r.at[8 + m], sibling)
            forwards[8 + m].start()
        gacc[...] = nt(x[k, r, :], weights[0, k])
        uacc[...] = nt(x[k, r, :], weights[1, k])
        for m in (2 * g, 2 * g + 1):
            for i, lane, width in ((0, lane_e, PAIR), (4, lane_s, 2 * PAIR), (8, lane_p, PAIR)):
                block = x.at[other, pl.ds(TOK * m, TOK), pl.ds(lane, width)]
                remote(block, block, f_s.at[i + m], f_r.at[i + m], sibling).wait_recv()
        gate = gacc[...] + nt(x[other, r, :], weights[0, other])
        up = uacc[...] + nt(x[other, r, :], weights[1, other])
        norm = x[k, r, pl.ds(lane_s + 128, 128)].astype(F32)
        norm = norm[:, 52:53] + norm[:, 53:54]
        gate, up = gate * norm, up * norm
        activated = (gate * jax.nn.sigmoid(1.702 * gate) * (up + 1.0)).astype(BF16)
        for i, lane in ((0, lane_o), (1, lane_s)):
            csend[i, r, :] = nn(activated, weights[2, other, :, pl.ds(lane, 2 * PAIR)]).astype(BF16)
            j = 2 * g + i
            pairs[j] = remote(
                csend.at[i, pl.ds(base, 256)], crecv.at[i, pl.ds(base, 256)], c_s.at[j], c_r.at[j], sibling
            )
            pairs[j].start()
        owne[r, :] = nn(activated, weights[2, k, :, pl.ds(lane_o, 2 * PAIR)])
        pairs[2 * g].wait_recv()
        for m in (2 * g, 2 * g + 1):
            rm = slice(TOK * m, TOK * (m + 1))
            owne[rm, :] = owne[rm, :] + crecv[0, rm, :].astype(F32)
            psend[rm, :] = owne[rm, pl.ds(pl.multiple_of(PAIR * (1 - b), 128), PAIR)].astype(BF16)
            piece = pl.ds(TOK * m, TOK)
            swaps[m] = remote(psend.at[piece], precv.at[piece], p_s.at[m], p_r.at[m], partner)
            swaps[m].start()
        owns[...] = nn(activated, weights[2, k, :, pl.ds(lane_s, 2 * PAIR)])
        pairs[2 * g + 1].wait_recv()
        for d in range(8 * g, 8 * g + 8):
            blk = slice(CAP * d, CAP * (d + 1))
            block = (owns[CAP * d - base : CAP * (d + 1) - base, :] + crecv[1, blk, :].astype(F32)).astype(BF16)
            if d == 0:
                ys[blk, :] = block
            else:
                yssend[blk, :] = block
                piece = pl.ds(CAP * d, CAP)
                back_s[d] = remote(yssend.at[piece], ys.at[piece], ys_s.at[d], ys_r.at[d], {"seq": behind[d]})
                back_s[d].start()
        if g == 0:
            make_gates()
        else:
            finish_group(0)
    maccs[...] = sum_shared(0)
    finish_group(1)

    unit = jnp.where(
        lax.broadcasted_iota(jnp.int32, (PAIR, PAIR), 0) == lax.broadcasted_iota(jnp.int32, (PAIR, PAIR), 1),
        jnp.float32(1.0), jnp.float32(0.0),
    ).astype(BF16)
    maccs[...] = maccs[...] + sum_shared(1)
    finals = []
    for q in range(2):
        turned = nt(unit, maccs[:, PAIR * q : PAIR * (q + 1)].astype(BF16))
        msends[2 * q : 2 * q + 2] = turned.astype(BF16).reshape(2, PAD, TOK)
        for j in (2 * q, 2 * q + 1):
            device = {"exp": 2 * (far_half + j) + k}
            finals.append(remote(msends.at[j], mrecv.at[2 + lax.rem(z, 4)], m_s.at[2 + j], m_r.at[2 + lax.rem(z, 4)], device))
            finals[j].start()
    for d in range(1, 16):
        back_e[d].wait_recv()
    macce[...] = nn(ghi[...], ye[...]) + nn(glo[...], ye[...])
    turned = nt(unit, macce[...].astype(BF16))
    msende[...] = turned.astype(BF16).reshape(2, PAD, TOK)
    to_mate = remote(msende.at[1 - b], mrecv.at[0], m_s.at[0], m_r.at[0], partner)
    to_pair = [
        remote(msende.at[j], mrecv.at[1], m_s.at[j], m_r.at[1], {"exp": 2 * (2 * group + j) + k}) for j in range(2)
    ]

    @pl.when(b == mid)
    def _():
        to_mate.start()
        mrecv[0] = msende[b]

    @pl.when(b != mid)
    def _():
        to_pair[0].start()
        to_pair[1].start()

    total = hid[...]
    for j in range(4):
        remote(msends.at[j], mrecv.at[2 + j], m_s.at[2 + j], m_r.at[2 + j], partner).wait_recv()
        total = total + mrecv[2 + j].astype(F32)
    remote(msende.at[0], mrecv.at[1], m_s.at[0], m_r.at[1], partner).wait_recv()

    @pl.when(b != mid)
    def _():
        to_mate.wait_recv()

    total = total + mrecv[1].astype(F32) + mrecv[0].astype(F32)
    out_ref[...] = total[0:SHARE, :].astype(BF16)

    @pl.when(b == mid)
    def _():
        to_mate.wait_send()

    @pl.when(b != mid)
    def _():
        to_pair[0].wait_send()
        to_pair[1].wait_send()

    halo.wait_send()
    for copy in first + second[1:] + squares[1:] + gather + logit_copies + to_e[1:] + to_s[1:]:
        copy.wait_send()
    for copy in passed + forwards + pairs + swaps + back_s[1:] + back_e[1:] + finals:
        copy.wait_send()


def vmem(*shape, dtype=BF16):
    return pltpu.VMEM(shape, dtype)


def body(
    queries, keyvals, sinks, out_proj, residual, norm_gain, router_weight, route_ids, expert_in, expert_out
):
    z = lax.axis_index("exp") // 2
    kv = lax.dynamic_slice(keyvals, (0, 0, 64 * z), (TOK, 2, 64)).reshape(TOK, TOK)
    local = pl.BlockSpec(memory_space=pltpu.VMEM)
    far = pl.BlockSpec(memory_space=pltpu.HBM)
    sems = lambda n: pltpu.SemaphoreType.DMA((n,))
    mixed = pl.pallas_call(
        kernel,
        out_shape=jax.ShapeDtypeStruct((SHARE, TOK), BF16),
        in_specs=[local, local, local, far, local, local, local, local, far, far],
        out_specs=local,
        scratch_shapes=[
            vmem(D, 256),
            vmem(3, UNITS, D),
            vmem(2 * TOK, TOK),
            vmem(TOK, 256),
            vmem(32, TOK, dtype=F32),
            vmem(ROWS, TOK),
            vmem(D + 16, TOK, dtype=F32),
            vmem(8, PAD, TOK),
            vmem(8, PAD, TOK),
            vmem(8, PAD, TOK),
            vmem(8, PAD, TOK),
            vmem(PAD, TOK, dtype=F32),
            vmem(PAD, TOK, dtype=F32),
            vmem(2 * PAIR, PAIR, dtype=jnp.int32),
            vmem(2 * PAIR, PAIR),
            vmem(3, 2, PAIR, HALF),
            vmem(1, TOK, dtype=F32),
            vmem(16, 1, TOK, dtype=F32),
            vmem(32, TOK, dtype=F32),
            vmem(32, TOK, dtype=F32),
            vmem(32, TOK, dtype=F32),
            vmem(8, 32, TOK, dtype=F32),
            vmem(8, PAD, TOK),
            vmem(ROWS, PAIR),
            vmem(ROWS, 2 * PAIR),
            vmem(2, ROWS, HALF),
            vmem(32, TOK, dtype=F32),
            vmem(ROWS, TOK),
            vmem(ROWS, TOK),
            vmem(TOK, ROWS),
            vmem(TOK, ROWS),
            vmem(256, PAIR, dtype=F32),
            vmem(256, PAIR, dtype=F32),
            vmem(256, 2 * PAIR, dtype=F32),
            vmem(ROWS, 2 * PAIR, dtype=F32),
            vmem(2, ROWS, 2 * PAIR),
            vmem(2, ROWS, 2 * PAIR),
            vmem(ROWS, PAIR),
            vmem(ROWS, PAIR),
            vmem(ROWS, 2 * PAIR),
            vmem(ROWS, PAIR),
            vmem(ROWS, 2 * PAIR),
            vmem(ROWS, PAIR),
            vmem(TOK, 2 * PAIR, dtype=F32),
            vmem(TOK, PAIR, dtype=F32),
            vmem(4, PAD, TOK),
            vmem(2, PAD, TOK),
            vmem(6, PAD, TOK),
            *(sems(n) for n in (3, 2, 8, 8, 8, 8, 16, 16, 8, 8, 6, 7)),
            *(sems(n) for n in (16, 16, 16, 16, 4, 4, 12, 12, 4, 4, 4, 4, 16, 16, 16, 16, 6, 6)),
        ],
        compiler_params=pltpu.CompilerParams(
            collective_id=0, has_side_effects=True, vmem_limit_bytes=56 * 2**20
        ),
        name="layer",
    )(
        queries,
        kv,
        sinks.reshape(1, 4),
        out_proj.T,
        residual.T,
        norm_gain.reshape(1, SHARE),
        router_weight.T,
        route_ids.T,
        jnp.transpose(expert_in[0], (1, 2, 0)),
        expert_out[0],
    )
    return mixed.T


def solution(mesh):
    return jax.shard_map(
        body,
        mesh=mesh,
        in_specs=(
            P("seq", "exp"),
            P("seq", None, None),
            P("exp"),
            P("exp", None),
            P("seq", "exp"),
            P("exp"),
            P("exp", None),
            P("seq", None),
            P(("seq", "exp"), None, None, None),
            P(("seq", "exp"), None, None),
        ),
        out_specs=P("seq", "exp"),
        check_vma=False,
    )
```

```python
import jax
import jax.numpy as jnp
from jax import lax
from jax.experimental import pallas as pl
from jax.experimental.pallas import tpu as pltpu
from jax.sharding import PartitionSpec as P

MESH = pl.DeviceIdType.MESH
F32, BF16 = jnp.float32, jnp.bfloat16
D = 2880
UNITS = 360
SHARE = 180
PAD = 192
PAIR = 2 * PAD
HALF = 8 * PAD
TOK = 128
CAP = 32
ROWS = 16 * CAP
EPS = 1e-05
STEPS = (
    (0, 0), (2, 2), (1, 2), (3, 2), (2, 1), (2, 3), (1, 1), (3, 3),
    (1, 3), (3, 1), (0, 2), (2, 0), (0, 1), (1, 0), (0, 3), (3, 0),
)
NT = (((1,), (1,)), ((), ()))


def nt(a, b):
    return lax.dot_general(a, b, NT, preferred_element_type=F32)


def nn(a, b):
    return jnp.dot(a, b, preferred_element_type=F32)


def kernel(
    q_hbm, kv_hbm, sink_hbm, proj_hbm, res_hbm, gain_hbm, router_hbm, route_hbm, win_hbm, wout_hbm,
    out_ref,
    q_ref, sink_ref, res_ref, gain_ref, router_ref, route_ref,
    proj, stage, kvall, wide, codes, pick, part, sibsend, sibrecv, rsend, rrecv, hid, mine,
    diff, sel, weights, sqsend, sqrecv, lgsend, lgsib, lgsum, lgrecv, xg, esend, ssend, x, gates, gthi, gtlo, ghi, glo,
    gacc, uacc, owns, owne, csend, crecv, psend, precv, yssend, yesend, ys, ye, maccs, macce, msends, msende, mrecv,
    load_sem, halo_sem, sib_s, sib_r, rs_s, rs_r, sq_s, sq_r, lg_s, lg_r, ag_s, ag_r,
    de_s, de_r, ds_s, ds_r, pf_s, pf_r, f_s, f_r, c_s, c_r, p_s, p_r, ys_s, ys_r, ye_s, ye_r, m_s, m_r,
):
    s, e = lax.axis_index("seq"), lax.axis_index("exp")
    z, k = e // 2, lax.rem(e, 2)
    h, b, mid = e // 8, lax.rem(z, 2), lax.rem(z // 2, 2)
    other = 1 - k
    sy, sx = s // 4, lax.rem(s, 4)
    ahead = [lax.rem(sy + dy, 4) * 4 + lax.rem(sx + dx, 4) for dy, dx in STEPS]
    behind = [lax.rem(sy + 4 - dy, 4) * 4 + lax.rem(sx + 4 - dx, 4) for dy, dx in STEPS]
    sibling = {"exp": 2 * z + other}
    zup = [lax.rem(z + d, 8) for d in range(8)]
    mate = z + 1 - 2 * b
    partner = {"exp": 2 * mate + k}
    far_half = 4 * (1 - h)
    group = 2 * h + b
    lane_e = pl.multiple_of(PAIR * group, 128)
    lane_p = pl.multiple_of(PAIR * (2 * h + 1 - b), 128)
    lane_s = pl.multiple_of(2 * PAIR * (1 - h), 128)
    lane_o = pl.multiple_of(2 * PAIR * h, 128)

    def remote(src, dst, send, recv, device):
        return pltpu.make_async_remote_copy(
            src_ref=src, dst_ref=dst, send_sem=send, recv_sem=recv, device_id=device, device_id_type=MESH
        )

    barrier = pltpu.get_barrier_semaphore()
    for d in range(1, 16):
        pl.semaphore_signal(barrier, inc=1, device_id={"seq": ahead[d]}, device_id_type=MESH)
        pl.semaphore_signal(barrier, inc=1, device_id={"exp": lax.rem(e + d, 16)}, device_id_type=MESH)
    small = [
        pltpu.make_async_copy(source, target, load_sem.at[3 + i])
        for i, (source, target) in enumerate((
            (route_hbm, route_ref), (kv_hbm, kvall.at[pl.ds(TOK, TOK)]), (q_hbm, q_ref), (sink_hbm, sink_ref),
            (res_hbm, res_ref), (gain_hbm, gain_ref), (router_hbm, router_ref),
        ))
    ]
    for copy in small:
        copy.start()
    load_proj = pltpu.make_async_copy(proj_hbm, proj, load_sem.at[0])
    load_in = pltpu.make_async_copy(win_hbm, stage.at[pl.ds(0, 2)], load_sem.at[1])
    load_out = pltpu.make_async_copy(wout_hbm, stage.at[2], load_sem.at[2])
    load_proj.start()
    load_in.start()
    load_out.start()

    small[0].wait()
    expert = lax.broadcasted_iota(jnp.int32, (32, TOK), 0)
    named = route_ref[0:1, :] == expert
    for j in range(1, 4):
        named = named | (route_ref[j : j + 1, :] == expert)
    named = jnp.where(named, jnp.float32(1.0), jnp.float32(0.0))
    before = jnp.where(
        lax.broadcasted_iota(jnp.int32, (TOK, TOK), 0) < lax.broadcasted_iota(jnp.int32, (TOK, TOK), 1),
        jnp.float32(1.0), jnp.float32(0.0),
    ).astype(BF16)
    rank = nn(named.astype(BF16), before)
    codes[...] = jnp.where(named > 0.0, rank, jnp.float32(-1.0))
    row = lax.broadcasted_iota(jnp.int32, (CAP, TOK), 0).astype(F32)
    for d in range(16):
        code = codes[pl.ds(2 * ahead[d] + h, 1), :]
        pick[CAP * d : CAP * (d + 1), :] = jnp.where(code == row, jnp.float32(1.0), jnp.float32(0.0)).astype(BF16)

    pl.semaphore_wait(barrier, 30)
    halo = remote(kv_hbm, kvall.at[pl.ds(0, TOK)], halo_sem.at[0], halo_sem.at[1], {"seq": lax.rem(s + 1, 16)})
    halo.start()
    weights[...] = jnp.zeros_like(weights)

    low = lax.broadcasted_iota(jnp.int32, (TOK, TOK), 1) < 64

    def sides(ref_part):
        kvf = ref_part.astype(F32)
        turned = pltpu.roll(kvf, 64, 1)
        zero = jnp.zeros_like(kvf)
        keys = [jnp.where(low, kvf, zero).astype(BF16), jnp.where(low, zero, turned).astype(BF16)]
        values = [jnp.where(low, turned, zero).astype(BF16), jnp.where(low, zero, kvf).astype(BF16)]
        return keys, values

    qpos = lax.broadcasted_iota(jnp.int32, (TOK, TOK), 0)
    kpos = lax.broadcasted_iota(jnp.int32, (TOK, TOK), 1)
    for i in (1, 2, 3):
        small[i].wait()
    keys, values = sides(kvall[TOK:, :])
    new = []
    for head in range(4):
        query = q_ref[:, 128 * (head // 2) : 128 * (head // 2 + 1)]
        score = nt(query, keys[head % 2]) * 0.125
        new.append(jnp.where(kpos <= qpos, jnp.exp(score), jnp.float32(0.0)))
    new_values = values
    halo.wait_recv()
    keys, values = sides(kvall[0:TOK, :])
    allowed = kpos > qpos + jnp.where(s > 0, 0, TOK)
    for pair in range(2):
        query = q_ref[:, 128 * pair : 128 * (pair + 1)]
        total = None
        for side in range(2):
            head = 2 * pair + side
            score = nt(query, keys[side]) * 0.125
            weight = jnp.where(allowed, jnp.exp(score), jnp.float32(0.0))
            denominator = jnp.sum(weight + new[head], axis=1, keepdims=True) + jnp.exp(
                sink_ref[0:1, head : head + 1]
            )
            scale = 1.0 / denominator
            term = nn((weight * scale).astype(BF16), values[side])
            term = term + nn((new[head] * scale).astype(BF16), new_values[side])
            total = term if total is None else total + term
        wide[:, 128 * pair : 128 * (pair + 1)] = total.astype(BF16)

    load_proj.wait()
    attended = wide[...]

    def project(i, carry):
        r = pl.multiple_of(i * 576, 576)
        part[pl.ds(r, 576), :] = nt(proj[pl.ds(r, 576), :], attended)
        return carry

    lax.fori_loop(0, 5, project, 0)
    part[D : D + 16, :] = jnp.zeros((16, TOK), F32)
    order = (4, 3, 5, 2, 6, 1, 7, 0)
    for i, d in enumerate(order):
        sibsend[i] = part[pl.ds(SHARE * (2 * zup[d] + other), PAD), :].astype(BF16)
        remote(sibsend.at[i], sibrecv.at[i], sib_s.at[0], sib_r.at[i // 4], sibling).start()
    for i, d in enumerate(order):
        if i % 4 == 0:
            block = pl.ds(i, 4)
            remote(sibsend.at[block], sibrecv.at[block], sib_s.at[0], sib_r.at[i // 4], sibling).wait_recv()
        pair_sum = part[pl.ds(SHARE * (2 * zup[d] + k), PAD), :] + sibrecv[i].astype(F32)
        if d == 0:
            mine[...] = pair_sum
        else:
            rsend[d] = pair_sum.astype(BF16)
            remote(rsend.at[d], rrecv.at[d], rs_s.at[0], rs_r.at[0], {"exp": 2 * zup[d] + k}).start()

    load_in.wait()
    ji = lax.broadcasted_iota(jnp.int32, (2 * PAIR, PAIR), 1)
    di = lax.broadcasted_iota(jnp.int32, (2 * PAIR, PAIR), 0) - ji
    di = jnp.where(ji < SHARE, di, -9999)
    ji2 = (ji >= PAD) & (ji < PAD + SHARE)
    di2 = lax.broadcasted_iota(jnp.int32, (2 * PAIR, PAIR), 0) - ji - (2 * SHARE - PAD)
    diff[...] = jnp.where(ji2, di2, di)

    def spread(first_matrix, count):
        def block(t, carry):
            q, p = t // 2, lax.rem(t, 2)
            start = 4 * SHARE * q + SHARE * p
            w0 = (start // 128) * 128
            sel[...] = jnp.where(diff[...] == start - w0, jnp.float32(1.0), jnp.float32(0.0)).astype(BF16)

            def matrix(m, c):
                window = stage[m, :, pl.ds(pl.multiple_of(w0, 128), 2 * PAIR)]
                lanes = pl.ds(pl.multiple_of(q * PAIR, 128), PAIR)
                weights[m, p, 0:UNITS, lanes] = nn(window, sel[...]).astype(BF16)
                return c

            return lax.fori_loop(first_matrix, first_matrix + count, matrix, carry)

        def last(m, c):
            window = stage[m, :, 2304:D]
            weights[m, 1, 0:UNITS, 3 * PAIR : 4 * PAIR] = nn(window, sel[0:576, :]).astype(BF16)
            return c

        lax.fori_loop(0, 7, block, 0)
        sel[...] = jnp.where(diff[...] == 36, jnp.float32(1.0), jnp.float32(0.0)).astype(BF16)
        lax.fori_loop(first_matrix, first_matrix + count, last, 0)

    spread(0, 2)

    total = mine[...]
    seven = pl.ds(1, 7)
    second = remote(rsend.at[seven], rrecv.at[seven], rs_s.at[0], rs_r.at[0], partner)
    second.wait_recv()
    for d in range(1, 8):
        total = total + rrecv[d].astype(F32)
    for i in (4, 5, 6):
        small[i].wait()
    hid[SHARE - 4 :, :] = jnp.zeros((PAD - SHARE + 4, TOK), F32)
    hid[0:SHARE, :] = res_ref[...].astype(F32) + total[0:SHARE, :]
    state = hid[...]
    diagonal = lax.broadcasted_iota(jnp.int32, (PAD, SHARE), 0) == lax.broadcasted_iota(jnp.int32, (PAD, SHARE), 1)
    gain = jnp.sum(jnp.where(diagonal, gain_ref[...], jnp.float32(0.0)), axis=1, keepdims=True)
    scaled = state * gain
    xg[z] = scaled.astype(BF16)
    sqsend[...] = jnp.sum(state * state, axis=0, keepdims=True)
    def gather(device, recv):
        remote(xg.at[z], xg.at[z], ag_s.at[0], ag_r.at[recv], device).start()

    gather(partner, 0)
    gather({"exp": 2 * (4 * h + 2 - mid) + k}, 1)
    for d in range(1, 16):
        device = {"exp": lax.rem(e + d, 16)}
        remote(sqsend, sqrecv.at[d], sq_s.at[0], sq_r.at[0], device).start()
    for i in range(2):
        gather({"exp": 2 * (far_half + 2 * i + b) + k}, 2 + mid)
    lgsend[...] = jnp.dot(
        router_ref[...], scaled[0:SHARE, :], precision=lax.Precision.HIGHEST, preferred_element_type=F32
    )
    lg_first = remote(lgsend, lgsib, lg_s.at[0], lg_r.at[0], sibling)
    lg_first.start()
    def arrived(slots, sem):
        remote(xg.at[slots], xg.at[slots], ag_s.at[0], ag_r.at[sem], partner).wait_recv()

    arrived(pl.ds(mate, 1), 0)

    @pl.when(b != mid)
    def _():
        arrived(pl.ds(4 * h + 2 * (1 - mid), 2), 1)

    features = xg[pl.ds(2 * group, 2)].reshape(PAIR, TOK)
    for g in range(4):
        r = slice(TOK * g, TOK * (g + 1))
        chosen = pick[r, :]
        esend[r, :] = nt(chosen, features).astype(BF16)
        for d in range(4 * g, 4 * g + 4):
            if d == 0:
                x[k, 0:CAP, pl.ds(lane_e, PAIR)] = esend[0:CAP, :]
            else:
                piece = pl.ds(CAP * d, CAP)
                target = x.at[k, piece, pl.ds(lane_e, PAIR)]
                remote(esend.at[piece], target, de_s.at[0], de_r.at[g], {"seq": ahead[d]}).start()

    def came(g, lane, width, recv):
        piece = pl.ds(CAP, TOK - CAP) if g == 0 else pl.ds(TOK * g, TOK)
        block = x.at[k, piece, pl.ds(lane, width)]
        remote(block, block, de_s.at[0], recv.at[g], partner).wait_recv()

    def forward(g, lane, width):
        block = x.at[k, pl.ds(TOK * g, TOK), pl.ds(lane, width)]
        remote(block, block, f_s.at[0], f_r.at[g // 2], sibling).start()

    def pass_on(g):
        came(g, lane_e, PAIR, de_r)
        block = x.at[k, pl.ds(TOK * g, TOK), pl.ds(lane_e, PAIR)]
        remote(block, block, pf_s.at[0], pf_r.at[g], partner).start()
        forward(g, lane_e, PAIR)

    for i in range(2):
        slot = far_half + 2 * i + b
        arrived(pl.ds(slot, 1), 2 + i)
        remote(xg.at[slot], xg.at[slot], ag_s.at[0], ag_r.at[4 + i], partner).start()
    pass_on(0)
    pass_on(1)
    lg_first.wait_recv()
    lgsum[...] = lgsend[...] + lgsib[...]
    for d in range(1, 8):
        remote(lgsum, lgrecv.at[d], lg_s.at[1], lg_r.at[1], {"exp": 2 * zup[d] + k}).start()
    lg_second = remote(lgrecv.at[seven], lgrecv.at[seven], lg_s.at[1], lg_r.at[1], partner)
    for i in range(2):
        arrived(pl.ds(far_half + 2 * i + 1 - b, 1), 4 + i)
    square = sqsend[...]
    fifteen = pl.ds(1, 15)
    squares = remote(sqrecv.at[fifteen], sqrecv.at[fifteen], sq_s.at[0], sq_r.at[0], partner)
    squares.wait_recv()
    for d in range(1, 16):
        square = square + sqrecv[d]
    factor = lax.rsqrt(square / D + EPS)
    high = factor.astype(BF16).astype(F32)
    ti = lax.broadcasted_iota(jnp.int32, (16, TOK), 0)
    spare = far_half + 1 - b
    tail = xg[spare, PAD - 16 :, :].astype(F32)
    tail = jnp.where(ti == 4, high, jnp.where(ti == 5, factor - high, tail))
    xg[spare, PAD - 16 :, :] = tail.astype(BF16)
    for g in range(4):
        r = slice(TOK * g, TOK * (g + 1))
        for q in range(2):
            features = xg[pl.ds(far_half + 2 * q, 2)].reshape(PAIR, TOK)
            ssend[r, PAIR * q : PAIR * (q + 1)] = nt(pick[r, :], features).astype(BF16)
        for d in range(4 * g, 4 * g + 4):
            if d == 0:
                x[k, 0:CAP, pl.ds(lane_s, 2 * PAIR)] = ssend[0:CAP, :]
            else:
                piece = pl.ds(CAP * d, CAP)
                target = x.at[k, piece, pl.ds(lane_s, 2 * PAIR)]
                remote(ssend.at[piece], target, ds_s.at[0], ds_r.at[g], {"seq": ahead[d]}).start()
    pass_on(2)
    pass_on(3)

    unit = jnp.where(
        lax.broadcasted_iota(jnp.int32, (TOK, TOK), 0) == lax.broadcasted_iota(jnp.int32, (TOK, TOK), 1),
        jnp.float32(1.0), jnp.float32(0.0),
    ).astype(BF16)

    load_out.wait()
    spread(2, 1)

    def make_gates():
        logits = lgsum[...]
        lg_second.wait_recv()
        for d in range(1, 8):
            logits = logits + lgrecv[d]
        raised = jnp.where(named > 0.0, jnp.exp(logits * factor), jnp.float32(0.0))
        gates[...] = raised / jnp.sum(raised, axis=0, keepdims=True)
        for d in range(16):
            r = slice(CAP * d, CAP * (d + 1))
            gate = gates[pl.ds(2 * ahead[d] + h, 1), :] * pick[r, :].astype(F32)
            gthi[r, :] = gate.astype(BF16)
            gtlo[r, :] = (gate - gate.astype(BF16).astype(F32)).astype(BF16)
        ghi[...] = nt(unit, gthi[...]).astype(BF16)
        glo[...] = nt(unit, gtlo[...]).astype(BF16)

    swaps = [None] * 4

    def finish_group(g):
        for d in range(8 * g, 8 * g + 8):
            if d % 4 == 0:
                swaps[d // 4].wait_recv()
            blk = slice(CAP * d, CAP * (d + 1))
            block = owne[blk, pl.ds(pl.multiple_of(PAIR * b, 128), PAIR)] + precv[blk, :].astype(F32)
            if d == 0:
                ye[blk, :] = block.astype(BF16)
            else:
                yesend[blk, :] = block.astype(BF16)
                piece = pl.ds(CAP * d, CAP)
                remote(yesend.at[piece], ye.at[piece], ye_s.at[0], ye_r.at[0], {"seq": behind[d]}).start()

    def sum_shared(g):
        r = slice(256 * g, 256 * (g + 1))
        piece = pl.ds(CAP, 256 - CAP) if g == 0 else pl.ds(256, 256)
        remote(yssend.at[piece], ys.at[piece], ys_s.at[0], ys_r.at[g], partner).wait_recv()
        return nn(ghi[:, r], ys[r, :]) + nn(glo[:, r], ys[r, :])

    for g in range(2):
        base = 256 * g
        r = slice(base, base + 256)
        for m in (2 * g, 2 * g + 1):
            came(m, lane_s, 2 * PAIR, ds_r)
            forward(m, lane_s, 2 * PAIR)
        for m in (2 * g, 2 * g + 1):
            block = x.at[k, pl.ds(TOK * m, TOK), pl.ds(lane_p, PAIR)]
            remote(block, block, pf_s.at[0], pf_r.at[m], partner).wait_recv()
            forward(m, lane_p, PAIR)
        gacc[...] = nt(x[k, r, :], weights[0, k])
        uacc[...] = nt(x[k, r, :], weights[1, k])
        block = x.at[other, pl.ds(base, 256)]
        remote(block, block, f_s.at[0], f_r.at[g], sibling).wait_recv()
        gate = gacc[...] + nt(x[other, r, :], weights[0, other])
        up = uacc[...] + nt(x[other, r, :], weights[1, other])
        norm = x[k, r, pl.ds(pl.multiple_of(lane_s + 128 * (2 - b), 128), 128)].astype(F32)
        lane = lax.broadcasted_iota(jnp.int32, (256, 128), 1) - jnp.where(b == 0, 116, 52)
        norm = jnp.sum(jnp.where((lane == 0) | (lane == 1), norm, jnp.float32(0.0)), axis=1, keepdims=True)
        gate, up = gate * norm, up * norm
        activated = (gate * jax.nn.sigmoid(1.702 * gate) * (up + 1.0)).astype(BF16)
        pairs = [None] * 2
        lanes = (lane_o, lane_s)
        sequence = (1, 0) if g == 0 else (0, 1)
        for i in sequence:
            csend[i, r, :] = nn(activated, weights[2, other, :, pl.ds(lanes[i], 2 * PAIR)]).astype(BF16)
            piece = pl.ds(base, 256)
            pairs[i] = remote(csend.at[i, piece], crecv.at[i, piece], c_s.at[0], c_r.at[2 * g + i], sibling)
            pairs[i].start()
        for i in sequence:
            product = nn(activated, weights[2, k, :, pl.ds(lanes[i], 2 * PAIR)])
            if i == 0:
                owne[r, :] = product
                pairs[0].wait_recv()
                for m in (2 * g, 2 * g + 1):
                    rm = slice(TOK * m, TOK * (m + 1))
                    owne[rm, :] = owne[rm, :] + crecv[0, rm, :].astype(F32)
                    psend[rm, :] = owne[rm, pl.ds(pl.multiple_of(PAIR * (1 - b), 128), PAIR)].astype(BF16)
                    piece = pl.ds(TOK * m, TOK)
                    swaps[m] = remote(psend.at[piece], precv.at[piece], p_s.at[0], p_r.at[m], partner)
                    swaps[m].start()
                continue
            owns[...] = product
            pairs[1].wait_recv()
            for d in range(8 * g, 8 * g + 8):
                blk = slice(CAP * d, CAP * (d + 1))
                block = owns[CAP * d - base : CAP * (d + 1) - base, :] + crecv[1, blk, :].astype(F32)
                if d == 0:
                    ys[blk, :] = block.astype(BF16)
                else:
                    yssend[blk, :] = block.astype(BF16)
                    piece = pl.ds(CAP * d, CAP)
                    remote(yssend.at[piece], ys.at[piece], ys_s.at[0], ys_r.at[g], {"seq": behind[d]}).start()
        if g == 0:
            make_gates()
        else:
            finish_group(0)
    maccs[...] = sum_shared(0)
    finish_group(1)

    unit = jnp.where(
        lax.broadcasted_iota(jnp.int32, (PAIR, PAIR), 0) == lax.broadcasted_iota(jnp.int32, (PAIR, PAIR), 1),
        jnp.float32(1.0), jnp.float32(0.0),
    ).astype(BF16)
    maccs[...] = maccs[...] + sum_shared(1)
    for q in range(2):
        turned = nt(unit, maccs[:, PAIR * q : PAIR * (q + 1)].astype(BF16))
        msends[2 * q : 2 * q + 2] = turned.astype(BF16).reshape(2, PAD, TOK)
        for j in (2 * q, 2 * q + 1):
            device = {"exp": 2 * (far_half + j) + k}
            remote(msends.at[j], mrecv.at[2 + lax.rem(z, 4)], m_s.at[0], m_r.at[2], device).start()
    others = pl.ds(CAP, ROWS - CAP)
    back_e = remote(yesend.at[others], ye.at[others], ye_s.at[0], ye_r.at[0], partner)
    back_e.wait_recv()
    macce[...] = nn(ghi[...], ye[...]) + nn(glo[...], ye[...])
    turned = nt(unit, macce[...].astype(BF16))
    msende[...] = turned.astype(BF16).reshape(2, PAD, TOK)
    to_mate = remote(msende.at[1 - b], mrecv.at[0], m_s.at[1], m_r.at[0], partner)

    @pl.when(b == mid)
    def _():
        to_mate.start()
        mrecv[0] = msende[b]

    @pl.when(b != mid)
    def _():
        for j in range(2):
            remote(msende.at[j], mrecv.at[1], m_s.at[1], m_r.at[1], {"exp": 2 * (2 * group + j) + k}).start()

    far_four = remote(msends, mrecv.at[pl.ds(2, 4)], m_s.at[0], m_r.at[2], partner)
    far_four.wait_recv()
    total = hid[...]
    for j in range(4):
        total = total + mrecv[2 + j].astype(F32)
    remote(msende.at[0], mrecv.at[1], m_s.at[1], m_r.at[1], partner).wait_recv()

    @pl.when(b != mid)
    def _():
        to_mate.wait_recv()

    total = total + mrecv[1].astype(F32) + mrecv[0].astype(F32)
    out_ref[...] = total[0:SHARE, :].astype(BF16)

    @pl.when(b == mid)
    def _():
        to_mate.wait_send()

    @pl.when(b != mid)
    def _():
        remote(msende, msende, m_s.at[1], m_r.at[1], partner).wait_send()

    def sent(ref, sem):
        remote(ref, ref, sem, sem, partner).wait_send()

    sent(sibsend, sib_s.at[0])
    sent(xg.at[pl.ds(0, 6)], ag_s.at[0])
    sent(esend.at[others], de_s.at[0])
    sent(ssend.at[others], ds_s.at[0])
    sent(esend, pf_s.at[0])
    sent(x.at[k], f_s.at[0])
    sent(csend, c_s.at[0])
    sent(psend, p_s.at[0])
    sent(yssend.at[others], ys_s.at[0])
    for copy in (halo, second, squares, lg_first, lg_second, back_e, far_four):
        copy.wait_send()


def vmem(*shape, dtype=BF16):
    return pltpu.VMEM(shape, dtype)


def body(
    queries, keyvals, sinks, out_proj, residual, norm_gain, router_weight, route_ids, expert_in, expert_out
):
    z = lax.axis_index("exp") // 2
    kv = lax.dynamic_slice(keyvals, (0, 0, 64 * z), (TOK, 2, 64)).reshape(TOK, TOK)
    local = pl.BlockSpec(memory_space=pltpu.VMEM)
    far = pl.BlockSpec(memory_space=pltpu.HBM)
    sems = lambda n: pltpu.SemaphoreType.DMA((n,))
    mixed = pl.pallas_call(
        kernel,
        out_shape=jax.ShapeDtypeStruct((SHARE, TOK), BF16),
        in_specs=[far] * 10,
        out_specs=local,
        scratch_shapes=[
            vmem(TOK, 256),
            vmem(1, 4, dtype=F32),
            vmem(SHARE, TOK),
            vmem(1, SHARE, dtype=F32),
            vmem(32, SHARE, dtype=F32),
            vmem(4, TOK, dtype=jnp.int32),
            vmem(D, 256),
            vmem(3, UNITS, D),
            vmem(2 * TOK, TOK),
            vmem(TOK, 256),
            vmem(32, TOK, dtype=F32),
            vmem(ROWS, TOK),
            vmem(D + 16, TOK, dtype=F32),
            vmem(8, PAD, TOK),
            vmem(8, PAD, TOK),
            vmem(8, PAD, TOK),
            vmem(8, PAD, TOK),
            vmem(PAD, TOK, dtype=F32),
            vmem(PAD, TOK, dtype=F32),
            vmem(2 * PAIR, PAIR, dtype=jnp.int32),
            vmem(2 * PAIR, PAIR),
            vmem(3, 2, PAIR, HALF),
            vmem(1, TOK, dtype=F32),
            vmem(16, 1, TOK, dtype=F32),
            vmem(32, TOK, dtype=F32),
            vmem(32, TOK, dtype=F32),
            vmem(32, TOK, dtype=F32),
            vmem(8, 32, TOK, dtype=F32),
            vmem(8, PAD, TOK),
            vmem(ROWS, PAIR),
            vmem(ROWS, 2 * PAIR),
            vmem(2, ROWS, HALF),
            vmem(32, TOK, dtype=F32),
            vmem(ROWS, TOK),
            vmem(ROWS, TOK),
            vmem(TOK, ROWS),
            vmem(TOK, ROWS),
            vmem(256, PAIR, dtype=F32),
            vmem(256, PAIR, dtype=F32),
            vmem(256, 2 * PAIR, dtype=F32),
            vmem(ROWS, 2 * PAIR, dtype=F32),
            vmem(2, ROWS, 2 * PAIR),
            vmem(2, ROWS, 2 * PAIR),
            vmem(ROWS, PAIR),
            vmem(ROWS, PAIR),
            vmem(ROWS, 2 * PAIR),
            vmem(ROWS, PAIR),
            vmem(ROWS, 2 * PAIR),
            vmem(ROWS, PAIR),
            vmem(TOK, 2 * PAIR, dtype=F32),
            vmem(TOK, PAIR, dtype=F32),
            vmem(4, PAD, TOK),
            vmem(2, PAD, TOK),
            vmem(6, PAD, TOK),
            *(sems(n) for n in (10, 2, 1, 2, 1, 1, 1, 1, 2, 2, 1, 6)),
            *(sems(n) for n in (1, 4, 1, 4, 1, 4, 1, 2, 1, 4, 1, 4, 1, 2, 1, 1, 2, 3)),
        ],
        compiler_params=pltpu.CompilerParams(
            collective_id=0, has_side_effects=True, vmem_limit_bytes=56 * 2**20
        ),
        name="layer",
    )(
        queries,
        kv,
        sinks.reshape(1, 4),
        out_proj.T,
        residual.T,
        norm_gain.reshape(1, SHARE),
        router_weight.T,
        route_ids.T,
        jnp.transpose(expert_in[0], (1, 2, 0)),
        expert_out[0],
    )
    return mixed.T


def solution(mesh):
    return jax.shard_map(
        body,
        mesh=mesh,
        in_specs=(
            P("seq", "exp"),
            P("seq", None, None),
            P("exp"),
            P("exp", None),
            P("seq", "exp"),
            P("exp"),
            P("exp", None),
            P("seq", None),
            P(("seq", "exp"), None, None, None),
            P(("seq", "exp"), None, None),
        ),
        out_specs=P("seq", "exp"),
        check_vma=False,
    )
```

```python
import jax
import jax.numpy as jnp
from jax import lax
from jax.experimental import pallas as pl
from jax.experimental.pallas import tpu as pltpu
from jax.sharding import PartitionSpec as P

MESH = pl.DeviceIdType.MESH
F32, BF16 = jnp.float32, jnp.bfloat16
D = 2880
UNITS = 360
SHARE = 180
PAD = 192
PAIR = 2 * PAD
HALF = 8 * PAD
TOK = 128
CAP = 32
ROWS = 16 * CAP
EPS = 1e-05
STEPS = (
    (0, 0), (2, 2), (1, 2), (3, 2), (2, 1), (2, 3), (1, 1), (3, 3),
    (1, 3), (3, 1), (0, 2), (2, 0), (0, 1), (1, 0), (0, 3), (3, 0),
)
NT = (((1,), (1,)), ((), ()))


def nt(a, b):
    return lax.dot_general(a, b, NT, preferred_element_type=F32)


def nn(a, b):
    return jnp.dot(a, b, preferred_element_type=F32)


def kernel(
    q_hbm, kv_hbm, sink_hbm, proj_hbm, res_hbm, gain_hbm, router_hbm, route_hbm, win_hbm, wout_hbm,
    out_ref,
    q_ref, sink_ref, res_ref, gain_ref, router_ref, route_ref,
    proj, stage, kvall, wide, codes, pick, part, sibsend, sibrecv, rsend, rrecv, hid, mine,
    diff, sel, weights, sqsend, sqrecv, lgsend, lgsib, lgsum, lgrecv, xg, esend, ssend, x, gates, gthi, gtlo, ghi, glo,
    gacc, uacc, owns, owne, csend, crecv, psend, precv, yssend, yesend, ys, ye, maccs, macce, msends, msende, mrecv,
    load_sem, halo_sem, sib_s, sib_r, rs_s, rs_r, sq_s, sq_r, lg_s, lg_r, ag_s, ag_r,
    de_s, de_r, ds_s, ds_r, pf_s, pf_r, f_s, f_r, c_s, c_r, p_s, p_r, ys_s, ys_r, ye_s, ye_r, m_s, m_r,
):
    s, e = lax.axis_index("seq"), lax.axis_index("exp")
    z, k = e // 2, lax.rem(e, 2)
    h, b, mid = e // 8, lax.rem(z, 2), lax.rem(z // 2, 2)
    other = 1 - k
    sy, sx = s // 4, lax.rem(s, 4)
    ahead = [lax.rem(sy + dy, 4) * 4 + lax.rem(sx + dx, 4) for dy, dx in STEPS]
    behind = [lax.rem(sy + 4 - dy, 4) * 4 + lax.rem(sx + 4 - dx, 4) for dy, dx in STEPS]
    sibling = {"exp": 2 * z + other}
    zup = [lax.rem(z + d, 8) for d in range(8)]
    mate = z + 1 - 2 * b
    partner = {"exp": 2 * mate + k}
    far_half = 4 * (1 - h)
    group = 2 * h + b
    lane_e = pl.multiple_of(PAIR * group, 128)
    lane_p = pl.multiple_of(PAIR * (2 * h + 1 - b), 128)
    lane_s = pl.multiple_of(2 * PAIR * (1 - h), 128)
    lane_o = pl.multiple_of(2 * PAIR * h, 128)

    def remote(src, dst, send, recv, device):
        return pltpu.make_async_remote_copy(
            src_ref=src, dst_ref=dst, send_sem=send, recv_sem=recv, device_id=device, device_id_type=MESH
        )

    barrier = pltpu.get_barrier_semaphore()
    for d in range(1, 16):
        pl.semaphore_signal(barrier, inc=1, device_id={"seq": ahead[d]}, device_id_type=MESH)
        pl.semaphore_signal(barrier, inc=1, device_id={"exp": lax.rem(e + d, 16)}, device_id_type=MESH)
    small = [
        pltpu.make_async_copy(source, target, load_sem.at[3 + i])
        for i, (source, target) in enumerate((
            (route_hbm, route_ref), (kv_hbm, kvall.at[pl.ds(TOK, TOK)]), (q_hbm, q_ref), (sink_hbm, sink_ref),
            (res_hbm, res_ref), (gain_hbm, gain_ref), (router_hbm, router_ref),
        ))
    ]
    for copy in small:
        copy.start()
    load_proj = pltpu.make_async_copy(proj_hbm, proj, load_sem.at[0])
    load_in = pltpu.make_async_copy(win_hbm, stage.at[pl.ds(0, 2)], load_sem.at[1])
    load_out = pltpu.make_async_copy(wout_hbm, stage.at[2], load_sem.at[2])
    load_proj.start()
    load_in.start()
    load_out.start()

    small[0].wait()
    expert = lax.broadcasted_iota(jnp.int32, (32, TOK), 0)
    named = route_ref[0:1, :] == expert
    for j in range(1, 4):
        named = named | (route_ref[j : j + 1, :] == expert)
    named = jnp.where(named, jnp.float32(1.0), jnp.float32(0.0))
    before = jnp.where(
        lax.broadcasted_iota(jnp.int32, (TOK, TOK), 0) < lax.broadcasted_iota(jnp.int32, (TOK, TOK), 1),
        jnp.float32(1.0), jnp.float32(0.0),
    ).astype(BF16)
    rank = nn(named.astype(BF16), before)
    codes[...] = jnp.where(named > 0.0, rank, jnp.float32(-1.0))
    row = lax.broadcasted_iota(jnp.int32, (CAP, TOK), 0).astype(F32)
    for d in range(16):
        code = codes[pl.ds(2 * ahead[d] + h, 1), :]
        pick[CAP * d : CAP * (d + 1), :] = jnp.where(code == row, jnp.float32(1.0), jnp.float32(0.0)).astype(BF16)

    pl.semaphore_wait(barrier, 30)
    halo = remote(kv_hbm, kvall.at[pl.ds(0, TOK)], halo_sem.at[0], halo_sem.at[1], {"seq": lax.rem(s + 1, 16)})
    halo.start()
    weights[...] = jnp.zeros_like(weights)

    low = lax.broadcasted_iota(jnp.int32, (TOK, TOK), 1) < 64

    def sides(ref_part):
        kvf = ref_part.astype(F32)
        turned = pltpu.roll(kvf, 64, 1)
        zero = jnp.zeros_like(kvf)
        keys = [jnp.where(low, kvf, zero).astype(BF16), jnp.where(low, zero, turned).astype(BF16)]
        values = [jnp.where(low, turned, zero).astype(BF16), jnp.where(low, zero, kvf).astype(BF16)]
        return keys, values

    qpos = lax.broadcasted_iota(jnp.int32, (TOK, TOK), 0)
    kpos = lax.broadcasted_iota(jnp.int32, (TOK, TOK), 1)
    for i in (1, 2, 3):
        small[i].wait()
    keys, values = sides(kvall[TOK:, :])
    new = []
    for head in range(4):
        query = q_ref[:, 128 * (head // 2) : 128 * (head // 2 + 1)]
        score = nt(query, keys[head % 2]) * 0.125
        new.append(jnp.where(kpos <= qpos, jnp.exp(score), jnp.float32(0.0)))
    new_values = values
    halo.wait_recv()
    keys, values = sides(kvall[0:TOK, :])
    allowed = kpos > qpos + jnp.where(s > 0, 0, TOK)
    for pair in range(2):
        query = q_ref[:, 128 * pair : 128 * (pair + 1)]
        total = None
        for side in range(2):
            head = 2 * pair + side
            score = nt(query, keys[side]) * 0.125
            weight = jnp.where(allowed, jnp.exp(score), jnp.float32(0.0))
            denominator = jnp.sum(weight + new[head], axis=1, keepdims=True) + jnp.exp(
                sink_ref[0:1, head : head + 1]
            )
            scale = 1.0 / denominator
            term = nn((weight * scale).astype(BF16), values[side])
            term = term + nn((new[head] * scale).astype(BF16), new_values[side])
            total = term if total is None else total + term
        wide[:, 128 * pair : 128 * (pair + 1)] = total.astype(BF16)

    load_proj.wait()
    attended = wide[...]

    def project(i, carry):
        r = pl.multiple_of(i * 576, 576)
        part[pl.ds(r, 576), :] = nt(proj[pl.ds(r, 576), :], attended)
        return carry

    lax.fori_loop(0, 5, project, 0)
    part[D : D + 16, :] = jnp.zeros((16, TOK), F32)
    order = (4, 3, 5, 2, 6, 1, 7, 0)
    for i, d in enumerate(order):
        sibsend[i] = part[pl.ds(SHARE * (2 * zup[d] + other), PAD), :].astype(BF16)
        remote(sibsend.at[i], sibrecv.at[i], sib_s.at[0], sib_r.at[i // 4], sibling).start()
    for i, d in enumerate(order):
        if i % 4 == 0:
            block = pl.ds(i, 4)
            remote(sibsend.at[block], sibrecv.at[block], sib_s.at[0], sib_r.at[i // 4], sibling).wait_recv()
        pair_sum = part[pl.ds(SHARE * (2 * zup[d] + k), PAD), :] + sibrecv[i].astype(F32)
        if d == 0:
            mine[...] = pair_sum
        else:
            rsend[d] = pair_sum.astype(BF16)
            remote(rsend.at[d], rrecv.at[d], rs_s.at[0], rs_r.at[0], {"exp": 2 * zup[d] + k}).start()

    load_in.wait()
    ji = lax.broadcasted_iota(jnp.int32, (2 * PAIR, PAIR), 1)
    di = lax.broadcasted_iota(jnp.int32, (2 * PAIR, PAIR), 0) - ji
    di = jnp.where(ji < SHARE, di, -9999)
    ji2 = (ji >= PAD) & (ji < PAD + SHARE)
    di2 = lax.broadcasted_iota(jnp.int32, (2 * PAIR, PAIR), 0) - ji - (2 * SHARE - PAD)
    diff[...] = jnp.where(ji2, di2, di)

    def spread(first_matrix, count):
        def block(t, carry):
            q, p = t // 2, lax.rem(t, 2)
            start = 4 * SHARE * q + SHARE * p
            w0 = (start // 128) * 128
            sel[...] = jnp.where(diff[...] == start - w0, jnp.float32(1.0), jnp.float32(0.0)).astype(BF16)

            def matrix(m, c):
                window = stage[m, :, pl.ds(pl.multiple_of(w0, 128), 2 * PAIR)]
                lanes = pl.ds(pl.multiple_of(q * PAIR, 128), PAIR)
                weights[m, p, 0:UNITS, lanes] = nn(window, sel[...]).astype(BF16)
                return c

            return lax.fori_loop(first_matrix, first_matrix + count, matrix, carry)

        def last(m, c):
            window = stage[m, :, 2304:D]
            weights[m, 1, 0:UNITS, 3 * PAIR : 4 * PAIR] = nn(window, sel[0:576, :]).astype(BF16)
            return c

        lax.fori_loop(0, 7, block, 0)
        sel[...] = jnp.where(diff[...] == 36, jnp.float32(1.0), jnp.float32(0.0)).astype(BF16)
        lax.fori_loop(first_matrix, first_matrix + count, last, 0)

    spread(0, 2)

    total = mine[...]
    seven = pl.ds(1, 7)
    second = remote(rsend.at[seven], rrecv.at[seven], rs_s.at[0], rs_r.at[0], partner)
    second.wait_recv()
    for d in range(1, 8):
        total = total + rrecv[d].astype(F32)
    for i in (4, 5, 6):
        small[i].wait()
    hid[SHARE - 4 :, :] = jnp.zeros((PAD - SHARE + 4, TOK), F32)
    hid[0:SHARE, :] = res_ref[...].astype(F32) + total[0:SHARE, :]
    state = hid[...]
    diagonal = lax.broadcasted_iota(jnp.int32, (PAD, SHARE), 0) == lax.broadcasted_iota(jnp.int32, (PAD, SHARE), 1)
    gain = jnp.sum(jnp.where(diagonal, gain_ref[...], jnp.float32(0.0)), axis=1, keepdims=True)
    scaled = state * gain
    xg[z] = scaled.astype(BF16)
    sqsend[...] = jnp.sum(state * state, axis=0, keepdims=True)
    def gather(device, recv):
        remote(xg.at[z], xg.at[z], ag_s.at[0], ag_r.at[recv], device).start()

    gather(partner, 0)
    gather({"exp": 2 * (4 * h + 2 - mid) + k}, 1)
    for i in range(2):
        gather({"exp": 2 * (far_half + 2 * i + b) + k}, 2 + mid)
    for d in range(1, 16):
        device = {"exp": lax.rem(e + d, 16)}
        remote(sqsend, sqrecv.at[d], sq_s.at[0], sq_r.at[0], device).start()
    lgsend[...] = jnp.dot(
        router_ref[...], scaled[0:SHARE, :], precision=lax.Precision.HIGHEST, preferred_element_type=F32
    )
    lg_first = remote(lgsend, lgsib, lg_s.at[0], lg_r.at[0], sibling)
    lg_first.start()
    def arrived(slots, sem):
        remote(xg.at[slots], xg.at[slots], ag_s.at[0], ag_r.at[sem], partner).wait_recv()

    arrived(pl.ds(mate, 1), 0)

    @pl.when(b != mid)
    def _():
        arrived(pl.ds(4 * h + 2 * (1 - mid), 2), 1)

    features = xg[pl.ds(2 * group, 2)].reshape(PAIR, TOK)
    for g in range(4):
        r = slice(TOK * g, TOK * (g + 1))
        chosen = pick[r, :]
        esend[r, :] = nt(chosen, features).astype(BF16)
        for d in range(4 * g, 4 * g + 4):
            if d == 0:
                x[k, 0:CAP, pl.ds(lane_e, PAIR)] = esend[0:CAP, :]
            else:
                piece = pl.ds(CAP * d, CAP)
                target = x.at[k, piece, pl.ds(lane_e, PAIR)]
                remote(esend.at[piece], target, de_s.at[0], de_r.at[g], {"seq": ahead[d]}).start()

    def came(g, lane, width, recv):
        piece = pl.ds(CAP, TOK - CAP) if g == 0 else pl.ds(TOK * g, TOK)
        block = x.at[k, piece, pl.ds(lane, width)]
        remote(block, block, de_s.at[0], recv.at[g], partner).wait_recv()

    def forward(g, lane, width):
        block = x.at[k, pl.ds(TOK * g, TOK), pl.ds(lane, width)]
        remote(block, block, f_s.at[0], f_r.at[g // 2], sibling).start()

    def pass_on(g):
        came(g, lane_e, PAIR, de_r)
        block = x.at[k, pl.ds(TOK * g, TOK), pl.ds(lane_e, PAIR)]
        remote(block, block, pf_s.at[0], pf_r.at[g], partner).start()
        forward(g, lane_e, PAIR)

    for i in range(2):
        slot = far_half + 2 * i + b
        arrived(pl.ds(slot, 1), 2 + i)
        remote(xg.at[slot], xg.at[slot], ag_s.at[0], ag_r.at[4 + i], partner).start()
    pass_on(0)
    pass_on(1)
    lg_first.wait_recv()
    lgsum[...] = lgsend[...] + lgsib[...]
    for d in range(1, 8):
        remote(lgsum, lgrecv.at[d], lg_s.at[1], lg_r.at[1], {"exp": 2 * zup[d] + k}).start()
    lg_second = remote(lgrecv.at[seven], lgrecv.at[seven], lg_s.at[1], lg_r.at[1], partner)
    for i in range(2):
        arrived(pl.ds(far_half + 2 * i + 1 - b, 1), 4 + i)
    square = sqsend[...]
    fifteen = pl.ds(1, 15)
    squares = remote(sqrecv.at[fifteen], sqrecv.at[fifteen], sq_s.at[0], sq_r.at[0], partner)
    squares.wait_recv()
    for d in range(1, 16):
        square = square + sqrecv[d]
    factor = lax.rsqrt(square / D + EPS)
    high = factor.astype(BF16).astype(F32)
    ti = lax.broadcasted_iota(jnp.int32, (16, TOK), 0)
    spare = far_half + 1 - b
    tail = xg[spare, PAD - 16 :, :].astype(F32)
    tail = jnp.where(ti == 4, high, jnp.where(ti == 5, factor - high, tail))
    xg[spare, PAD - 16 :, :] = tail.astype(BF16)
    for g in range(4):
        r = slice(TOK * g, TOK * (g + 1))
        for q in range(2):
            features = xg[pl.ds(far_half + 2 * q, 2)].reshape(PAIR, TOK)
            ssend[r, PAIR * q : PAIR * (q + 1)] = nt(pick[r, :], features).astype(BF16)
        for d in range(4 * g, 4 * g + 4):
            if d == 0:
                x[k, 0:CAP, pl.ds(lane_s, 2 * PAIR)] = ssend[0:CAP, :]
            else:
                piece = pl.ds(CAP * d, CAP)
                target = x.at[k, piece, pl.ds(lane_s, 2 * PAIR)]
                remote(ssend.at[piece], target, ds_s.at[0], ds_r.at[g], {"seq": ahead[d]}).start()
    pass_on(2)
    pass_on(3)

    unit = jnp.where(
        lax.broadcasted_iota(jnp.int32, (TOK, TOK), 0) == lax.broadcasted_iota(jnp.int32, (TOK, TOK), 1),
        jnp.float32(1.0), jnp.float32(0.0),
    ).astype(BF16)

    load_out.wait()
    spread(2, 1)

    def make_gates():
        logits = lgsum[...]
        lg_second.wait_recv()
        for d in range(1, 8):
            logits = logits + lgrecv[d]
        raised = jnp.where(named > 0.0, jnp.exp(logits * factor), jnp.float32(0.0))
        gates[...] = raised / jnp.sum(raised, axis=0, keepdims=True)
        for d in range(16):
            r = slice(CAP * d, CAP * (d + 1))
            gate = gates[pl.ds(2 * ahead[d] + h, 1), :] * pick[r, :].astype(F32)
            gthi[r, :] = gate.astype(BF16)
            gtlo[r, :] = (gate - gate.astype(BF16).astype(F32)).astype(BF16)
        ghi[...] = nt(unit, gthi[...]).astype(BF16)
        glo[...] = nt(unit, gtlo[...]).astype(BF16)

    swaps = [None] * 4

    def finish_group(g):
        for d in range(8 * g, 8 * g + 8):
            if d % 4 == 0:
                swaps[d // 4].wait_recv()
            blk = slice(CAP * d, CAP * (d + 1))
            block = owne[blk, pl.ds(pl.multiple_of(PAIR * b, 128), PAIR)] + precv[blk, :].astype(F32)
            if d == 0:
                ye[blk, :] = block.astype(BF16)
            else:
                yesend[blk, :] = block.astype(BF16)
                piece = pl.ds(CAP * d, CAP)
                remote(yesend.at[piece], ye.at[piece], ye_s.at[0], ye_r.at[0], {"seq": behind[d]}).start()

    def sum_shared(g):
        r = slice(256 * g, 256 * (g + 1))
        piece = pl.ds(CAP, 256 - CAP) if g == 0 else pl.ds(256, 256)
        remote(yssend.at[piece], ys.at[piece], ys_s.at[0], ys_r.at[g], partner).wait_recv()
        return nn(ghi[:, r], ys[r, :]) + nn(glo[:, r], ys[r, :])

    for g in range(2):
        base = 256 * g
        r = slice(base, base + 256)
        for m in (2 * g, 2 * g + 1):
            came(m, lane_s, 2 * PAIR, ds_r)
            forward(m, lane_s, 2 * PAIR)
        for m in (2 * g, 2 * g + 1):
            block = x.at[k, pl.ds(TOK * m, TOK), pl.ds(lane_p, PAIR)]
            remote(block, block, pf_s.at[0], pf_r.at[m], partner).wait_recv()
            forward(m, lane_p, PAIR)
        gacc[...] = nt(x[k, r, :], weights[0, k])
        uacc[...] = nt(x[k, r, :], weights[1, k])
        block = x.at[other, pl.ds(base, 256)]
        remote(block, block, f_s.at[0], f_r.at[g], sibling).wait_recv()
        gate = gacc[...] + nt(x[other, r, :], weights[0, other])
        up = uacc[...] + nt(x[other, r, :], weights[1, other])
        norm = x[k, r, pl.ds(pl.multiple_of(lane_s + 128 * (2 - b), 128), 128)].astype(F32)
        lane = lax.broadcasted_iota(jnp.int32, (256, 128), 1) - jnp.where(b == 0, 116, 52)
        norm = jnp.sum(jnp.where((lane == 0) | (lane == 1), norm, jnp.float32(0.0)), axis=1, keepdims=True)
        gate, up = gate * norm, up * norm
        activated = (gate * jax.nn.sigmoid(1.702 * gate) * (up + 1.0)).astype(BF16)
        pairs = [None] * 2
        lanes = (lane_o, lane_s)
        sequence = (1, 0) if g == 0 else (0, 1)
        for i in sequence:
            csend[i, r, :] = nn(activated, weights[2, other, :, pl.ds(lanes[i], 2 * PAIR)]).astype(BF16)
            piece = pl.ds(base, 256)
            pairs[i] = remote(csend.at[i, piece], crecv.at[i, piece], c_s.at[0], c_r.at[2 * g + i], sibling)
            pairs[i].start()
        for i in sequence:
            product = nn(activated, weights[2, k, :, pl.ds(lanes[i], 2 * PAIR)])
            if i == 0:
                owne[r, :] = product
                pairs[0].wait_recv()
                for m in (2 * g, 2 * g + 1):
                    rm = slice(TOK * m, TOK * (m + 1))
                    owne[rm, :] = owne[rm, :] + crecv[0, rm, :].astype(F32)
                    psend[rm, :] = owne[rm, pl.ds(pl.multiple_of(PAIR * (1 - b), 128), PAIR)].astype(BF16)
                    piece = pl.ds(TOK * m, TOK)
                    swaps[m] = remote(psend.at[piece], precv.at[piece], p_s.at[0], p_r.at[m], partner)
                    swaps[m].start()
                continue
            owns[...] = product
            pairs[1].wait_recv()
            for d in range(8 * g, 8 * g + 8):
                blk = slice(CAP * d, CAP * (d + 1))
                block = owns[CAP * d - base : CAP * (d + 1) - base, :] + crecv[1, blk, :].astype(F32)
                if d == 0:
                    ys[blk, :] = block.astype(BF16)
                else:
                    yssend[blk, :] = block.astype(BF16)
                    piece = pl.ds(CAP * d, CAP)
                    remote(yssend.at[piece], ys.at[piece], ys_s.at[0], ys_r.at[g], {"seq": behind[d]}).start()
        if g == 1:
            finish_group(0)
            make_gates()
    maccs[...] = sum_shared(0)
    finish_group(1)

    unit = jnp.where(
        lax.broadcasted_iota(jnp.int32, (PAIR, PAIR), 0) == lax.broadcasted_iota(jnp.int32, (PAIR, PAIR), 1),
        jnp.float32(1.0), jnp.float32(0.0),
    ).astype(BF16)
    maccs[...] = maccs[...] + sum_shared(1)
    for q in range(2):
        turned = nt(unit, maccs[:, PAIR * q : PAIR * (q + 1)].astype(BF16))
        msends[2 * q : 2 * q + 2] = turned.astype(BF16).reshape(2, PAD, TOK)
        for j in (2 * q, 2 * q + 1):
            device = {"exp": 2 * (far_half + j) + k}
            remote(msends.at[j], mrecv.at[2 + lax.rem(z, 4)], m_s.at[0], m_r.at[2], device).start()
    others = pl.ds(CAP, ROWS - CAP)
    back_e = remote(yesend.at[others], ye.at[others], ye_s.at[0], ye_r.at[0], partner)
    back_e.wait_recv()
    macce[...] = nn(ghi[...], ye[...]) + nn(glo[...], ye[...])
    turned = nt(unit, macce[...].astype(BF16))
    msende[...] = turned.astype(BF16).reshape(2, PAD, TOK)
    to_mate = remote(msende.at[1 - b], mrecv.at[0], m_s.at[1], m_r.at[0], partner)

    @pl.when(b == mid)
    def _():
        to_mate.start()
        mrecv[0] = msende[b]

    @pl.when(b != mid)
    def _():
        for j in range(2):
            remote(msende.at[j], mrecv.at[1], m_s.at[1], m_r.at[1], {"exp": 2 * (2 * group + j) + k}).start()

    far_four = remote(msends, mrecv.at[pl.ds(2, 4)], m_s.at[0], m_r.at[2], partner)
    far_four.wait_recv()
    total = hid[...]
    for j in range(4):
        total = total + mrecv[2 + j].astype(F32)
    remote(msende.at[0], mrecv.at[1], m_s.at[1], m_r.at[1], partner).wait_recv()

    @pl.when(b != mid)
    def _():
        to_mate.wait_recv()

    total = total + mrecv[1].astype(F32) + mrecv[0].astype(F32)
    out_ref[...] = total[0:SHARE, :].astype(BF16)

    @pl.when(b == mid)
    def _():
        to_mate.wait_send()

    @pl.when(b != mid)
    def _():
        remote(msende, msende, m_s.at[1], m_r.at[1], partner).wait_send()

    def sent(ref, sem):
        remote(ref, ref, sem, sem, partner).wait_send()

    sent(sibsend, sib_s.at[0])
    sent(xg.at[pl.ds(0, 6)], ag_s.at[0])
    sent(esend.at[others], de_s.at[0])
    sent(ssend.at[others], ds_s.at[0])
    sent(esend, pf_s.at[0])
    sent(x.at[k], f_s.at[0])
    sent(csend, c_s.at[0])
    sent(psend, p_s.at[0])
    sent(yssend.at[others], ys_s.at[0])
    for copy in (halo, second, squares, lg_first, lg_second, back_e, far_four):
        copy.wait_send()


def vmem(*shape, dtype=BF16):
    return pltpu.VMEM(shape, dtype)


def body(
    queries, keyvals, sinks, out_proj, residual, norm_gain, router_weight, route_ids, expert_in, expert_out
):
    z = lax.axis_index("exp") // 2
    kv = lax.dynamic_slice(keyvals, (0, 0, 64 * z), (TOK, 2, 64)).reshape(TOK, TOK)
    local = pl.BlockSpec(memory_space=pltpu.VMEM)
    far = pl.BlockSpec(memory_space=pltpu.HBM)
    sems = lambda n: pltpu.SemaphoreType.DMA((n,))
    mixed = pl.pallas_call(
        kernel,
        out_shape=jax.ShapeDtypeStruct((SHARE, TOK), BF16),
        in_specs=[far] * 10,
        out_specs=local,
        scratch_shapes=[
            vmem(TOK, 256),
            vmem(1, 4, dtype=F32),
            vmem(SHARE, TOK),
            vmem(1, SHARE, dtype=F32),
            vmem(32, SHARE, dtype=F32),
            vmem(4, TOK, dtype=jnp.int32),
            vmem(D, 256),
            vmem(3, UNITS, D),
            vmem(2 * TOK, TOK),
            vmem(TOK, 256),
            vmem(32, TOK, dtype=F32),
            vmem(ROWS, TOK),
            vmem(D + 16, TOK, dtype=F32),
            vmem(8, PAD, TOK),
            vmem(8, PAD, TOK),
            vmem(8, PAD, TOK),
            vmem(8, PAD, TOK),
            vmem(PAD, TOK, dtype=F32),
            vmem(PAD, TOK, dtype=F32),
            vmem(2 * PAIR, PAIR, dtype=jnp.int32),
            vmem(2 * PAIR, PAIR),
            vmem(3, 2, PAIR, HALF),
            vmem(1, TOK, dtype=F32),
            vmem(16, 1, TOK, dtype=F32),
            vmem(32, TOK, dtype=F32),
            vmem(32, TOK, dtype=F32),
            vmem(32, TOK, dtype=F32),
            vmem(8, 32, TOK, dtype=F32),
            vmem(8, PAD, TOK),
            vmem(ROWS, PAIR),
            vmem(ROWS, 2 * PAIR),
            vmem(2, ROWS, HALF),
            vmem(32, TOK, dtype=F32),
            vmem(ROWS, TOK),
            vmem(ROWS, TOK),
            vmem(TOK, ROWS),
            vmem(TOK, ROWS),
            vmem(256, PAIR, dtype=F32),
            vmem(256, PAIR, dtype=F32),
            vmem(256, 2 * PAIR, dtype=F32),
            vmem(ROWS, 2 * PAIR, dtype=F32),
            vmem(2, ROWS, 2 * PAIR),
            vmem(2, ROWS, 2 * PAIR),
            vmem(ROWS, PAIR),
            vmem(ROWS, PAIR),
            vmem(ROWS, 2 * PAIR),
            vmem(ROWS, PAIR),
            vmem(ROWS, 2 * PAIR),
            vmem(ROWS, PAIR),
            vmem(TOK, 2 * PAIR, dtype=F32),
            vmem(TOK, PAIR, dtype=F32),
            vmem(4, PAD, TOK),
            vmem(2, PAD, TOK),
            vmem(6, PAD, TOK),
            *(sems(n) for n in (10, 2, 1, 2, 1, 1, 1, 1, 2, 2, 1, 6)),
            *(sems(n) for n in (1, 4, 1, 4, 1, 4, 1, 2, 1, 4, 1, 4, 1, 2, 1, 1, 2, 3)),
        ],
        compiler_params=pltpu.CompilerParams(
            collective_id=0, has_side_effects=True, vmem_limit_bytes=56 * 2**20
        ),
        name="layer",
    )(
        queries,
        kv,
        sinks.reshape(1, 4),
        out_proj.T,
        residual.T,
        norm_gain.reshape(1, SHARE),
        router_weight.T,
        route_ids.T,
        jnp.transpose(expert_in[0], (1, 2, 0)),
        expert_out[0],
    )
    return mixed.T


def solution(mesh):
    return jax.shard_map(
        body,
        mesh=mesh,
        in_specs=(
            P("seq", "exp"),
            P("seq", None, None),
            P("exp"),
            P("exp", None),
            P("seq", "exp"),
            P("exp"),
            P("exp", None),
            P("seq", None),
            P(("seq", "exp"), None, None, None),
            P(("seq", "exp"), None, None),
        ),
        out_specs=P("seq", "exp"),
        check_vma=False,
    )
```
